512 devices in a mesh: sector: 8 (over y), term: 64 (over x, z, core).
Axes of the slice: x: 4, y: 8, z: 8, core: 2. Of those that a mesh axis runs over, the one named last changes fastest.
Arguments:
- wave_in: bfloat16 [16, 1024, 256], P('sector'), may hold values from -6 to 6
- left_env: bfloat16 [16, 192, 1024, 256], P('sector', 'term'), may hold values from -0.1875 to 0.1875
- right_env: bfloat16 [16, 192, 256, 64], P('sector', 'term'), may hold values from -0.375 to 0.375
- shift_map: int32 [48, 16], replicated, may hold values from 0 to 15
- live_rows: int32 [16], replicated, may hold values from 512 to 1024
Outputs:
- isometry: bfloat16 [16, 1024, 256], P('sector', 'term')
- env_next: bfloat16 [16, 192, 256, 64], P('sector', 'term')
The draws below stay inside these ranges and needn't reach their ends.
All inputs are finite; a program needn't handle non-finite values.
Results may differ from the reference program's by a relative error of at most 0.014.
Values may be sent and summed in bfloat16 or wider, within the bound.
A program may use at most 64 MiB of HBM per device.

```python
import math
import jax
import jax.numpy as jnp
from jax import lax

S = 16
TERMS = 48
LEFT_ROWS = 1024
DR = 256
RSL = 4
STEPS = 8
PAIRS = 192
PAIR_DEV = 3
DLR = 256
DRR = 64


def place_ends(values, stream_key, smallest, largest):
    place = [jax.random.randint(jax.random.fold_in(stream_key, axis), (), 0, length) for axis, length in enumerate(values.shape)]
    main_axis = values.shape.index(max(values.shape))
    next_to = place[:main_axis] + [(place[main_axis] + 1) % values.shape[main_axis]] + place[main_axis + 1:]
    return values.at[tuple(place)].set(smallest).at[tuple(next_to)].set(largest)


def block_levels(rng, shape, split, low, largest):
    level = 1.0
    for dim, parts in split:
        steps = jax.random.uniform(jax.random.fold_in(jax.random.fold_in(rng, 6), dim), (parts,), jnp.float32, low / len(split), largest / len(split))
        level = level * jnp.repeat(jnp.exp(steps), shape[dim] // parts).reshape((-1,) + (1,) * (len(shape) - 1 - dim))
    return level


def scatter_about(key, shape, spread, bound, split=(), held_as=jnp.bfloat16):
    entries = spread * jax.random.normal(key, shape, jnp.float32)
    if split:
        entries = entries * block_levels(key, shape, split, -0.22, 0.18)
    return jnp.clip(entries, -bound, bound).astype(held_as)


def setup_inputs(seed: int = 0) -> dict:
    streams_of = jax.random.split(jax.random.key(seed), 6)
    return {
        "wave_in": scatter_about(streams_of[0], (S, LEFT_ROWS, DR), 1.0, 6.0, ((0, 8),)),
        "left_env": scatter_about(streams_of[1], (S, PAIRS, LEFT_ROWS, DLR), LEFT_ROWS ** -0.5, 0.1875, ((0, 8), (1, 64))),
        "right_env": scatter_about(streams_of[2], (S, PAIRS, DR, DRR), DR ** -0.5, 0.375, ((0, 8), (1, 64))),
        "shift_map": place_ends(jax.random.randint(streams_of[3], (TERMS, S), 0, S), jax.random.fold_in(streams_of[3], 1), 0, S - 1).astype(jnp.int32),
        "live_rows": place_ends(jax.random.randint(streams_of[4], (S,), LEFT_ROWS // 2, LEFT_ROWS + 1), jax.random.fold_in(streams_of[4], 1), LEFT_ROWS // 2, LEFT_ROWS).astype(jnp.int32),
    }


step_size = 0.15
epsilon = 1e-06
highest = lax.Precision.HIGHEST

def full_blocks(stacked, per_device):
    width_rows = stacked.shape[1]
    width_cols = stacked.shape[2]
    blocks = stacked.reshape(TERMS // per_device, RSL, per_device, width_rows, width_cols)
    blocks = jnp.transpose(blocks, (0, 2, 3, 1, 4))
    return blocks.reshape(TERMS, width_rows, RSL * width_cols)

def pair_layout(matrices, per_device):
    width_rows = matrices.shape[1]
    width_cols = matrices.shape[2] // RSL
    blocks = matrices.reshape(TERMS // per_device, per_device, width_rows, RSL, width_cols)
    blocks = jnp.transpose(blocks, (0, 3, 1, 2, 4))
    return blocks.reshape(TERMS * RSL, width_rows, width_cols)

def reference(wave_in, left_env, right_env, shift_map, live_rows):
    identity = jnp.eye(DR, dtype=jnp.float32)
    row_ids = jnp.arange(LEFT_ROWS, dtype=jnp.int32)

    def update(sector):
        left_complete = full_blocks(left_env[sector], PAIR_DEV).astype(jnp.float32)
        right_complete = full_blocks(right_env[sector], PAIR_DEV).astype(jnp.float32)
        sources = shift_map[:, sector]
        selected_block = wave_in[sources].astype(jnp.float32)
        operator_applied = jnp.einsum('zgo,zoy->zgy', selected_block, right_complete).astype(jnp.bfloat16)
        sigma_block_sum = jnp.einsum('hwm,hmx->wx', left_complete, operator_applied.astype(jnp.float32))
        live_mask = row_ids[:, None] < live_rows[sector]
        updated = jnp.where(live_mask, wave_in[sector].astype(jnp.float32) - step_size * sigma_block_sum, 0.0)
        gram_sum = jnp.dot(updated.T, updated, precision=highest)
        trace_sum = jnp.trace(gram_sum) + epsilon
        root_part = gram_sum / trace_sum
        inverse_part = identity
        for ns_step in range(STEPS):
            ns_factor = 1.5 * identity - 0.5 * jnp.dot(inverse_part, root_part, precision=highest)
            root_part = jnp.dot(root_part, ns_factor, precision=highest)
            inverse_part = jnp.dot(ns_factor, inverse_part, precision=highest)
        result = jnp.dot(updated, inverse_part, precision=highest) * jnp.sqrt(LEFT_ROWS / trace_sum)
        return result.astype(jnp.bfloat16)
    isometry = lax.map(update, jnp.arange(S, dtype=jnp.int32))

    def renorm(sector):
        left_complete = full_blocks(left_env[sector], PAIR_DEV).astype(jnp.float32)
        projected_wave = jnp.einsum('ia,tib->tab', isometry[sector].astype(jnp.float32), left_complete).astype(jnp.bfloat16)
        selected_block = isometry[shift_map[:, sector]].astype(jnp.float32)
        environment_block = jnp.einsum('zgo,zoy->zgy', projected_wave.astype(jnp.float32), selected_block) / math.sqrt(LEFT_ROWS)
        return pair_layout(environment_block.astype(jnp.bfloat16), PAIR_DEV)
    env_next = lax.map(renorm, jnp.arange(S, dtype=jnp.int32))
    return (isometry, env_next)
```

```python
import jax
import jax.numpy as jnp
from jax import lax
from jax.experimental import pallas as pl
from jax.experimental.pallas import tpu as pltpu
from jax.sharding import Mesh
from jax.sharding import PartitionSpec as P

STEPS = 8
NY, NX, NZ = 8, 4, 8
ROWS, COLS, HALF = 1024, 256, 128
TERM = ("x", "z", "core")
STEP_SIZE = 0.15
EPSILON = 1e-06
MESH = pl.DeviceIdType.MESH
F32, BF16 = jnp.float32, jnp.bfloat16
FAR_FIRST = (4, 3, 5, 2, 6, 1, 7, 0)


def dot(a, b):
    return jnp.dot(a, b, preferred_element_type=F32)


def dot_over_rows(a, b):
    return lax.dot_general(a, b, (((0,), (0,)), ((), ())), preferred_element_type=F32)


def two_parts(a):
    high = a.astype(BF16)
    return high, (a - high.astype(F32)).astype(BF16)


def dot3(a, b):
    return dot(a[0], b[0]) + (dot(a[0], b[1]) + dot(a[1], b[0]))


def remote(src, dst, send, recv, to):
    return pltpu.make_async_remote_copy(
        src_ref=src, dst_ref=dst, send_sem=send, recv_sem=recv, device_id=to, device_id_type=MESH
    )


class Gather:
    def __init__(self, pos, blocks, sems):
        self.pos, self.blocks = pos, blocks
        self.y_send, self.y_recv, self.x_send, self.x_recv = sems
        self.half = lax.rem(pos["x"], 2)
        self.started = []

    def place(self, way, d, j, half):
        y, core = self.pos["sector"], self.pos["core"]
        step = d if way == 0 else NY - d
        sector = core if j == 0 else 1 - core
        index = 2 * lax.rem(y - step + 2 * NY, NY) + sector
        return self.blocks.at[index, pl.ds(pl.multiple_of(half * HALF, HALF), HALF), :]

    def to_y(self, way):
        y = self.pos["sector"]
        return {**self.pos, "sector": lax.rem(y + (1 if way == 0 else NY - 1), NY)}

    def to_x(self, j):
        x = self.pos["x"]
        return {**self.pos, "x": lax.rem(x + (1 if j == 0 else NX - 1), NX)}

    def go(self, copy):
        copy.start()
        self.started.append(copy)

    def start(self, j, source):
        for way in (0, 1):
            self.go(
                remote(
                    source,
                    self.place(way, 0, j, self.half),
                    self.y_send.at[way, 0, j],
                    self.y_recv.at[way, 0, j],
                    self.to_y(way),
                )
            )

    def arrive(self, d):
        for j in (0, 1):
            for way in (0, 1):
                if d == 4 and j != way:
                    continue
                block = self.place(way, d, j, self.half)
                remote(
                    block,
                    block,
                    self.y_send.at[way, d - 1, j],
                    self.y_recv.at[way, d - 1, j],
                    self.to_y(way),
                ).wait_recv()
                if d < 3 or (d == 3 and j == way):
                    self.go(
                        remote(
                            block,
                            block,
                            self.y_send.at[way, d, j],
                            self.y_recv.at[way, d, j],
                            self.to_y(way),
                        )
                    )
                self.go(
                    remote(
                        block,
                        block,
                        self.x_send.at[way, d - 1, j],
                        self.x_recv.at[way, d - 1, j],
                        self.to_x(j),
                    )
                )

    def finish(self):
        for d in (1, 2, 3, 4):
            for j in (0, 1):
                for way in (0, 1):
                    if d == 4 and j != way:
                        continue
                    block = self.place(way, d, j, 1 - self.half)
                    remote(
                        block,
                        block,
                        self.x_send.at[way, d - 1, j],
                        self.x_recv.at[way, d - 1, j],
                        self.to_x(j),
                    ).wait_recv()


def kernel(
    shift,
    live,
    wave,
    left,
    right,
    iso_out,
    env_out,
    left_v,
    wave_v,
    wave_all,
    right_all,
    right_full,
    applied,
    sib_out,
    sib_in,
    sigma,
    x_out,
    x_own,
    x_in,
    z_out,
    z_own,
    z_in,
    total,
    u_high,
    u_low,
    root,
    inverse,
    iso,
    iso_all,
    front,
    e_out,
    e_in,
    e_own,
    ez_out,
    ez_in,
    local_sem,
    r_send,
    r_recv,
    sib_send,
    sib_recv,
    xs_send,
    xs_recv,
    zs_send,
    zs_recv,
    gz_send,
    gz_recv,
    gx_send,
    gx_recv,
    i_send,
    i_recv,
    e_send,
    e_recv,
    ez_send,
    ez_recv,
    *ring_sems,
):
    y, x, z, core = (lax.axis_index(a) for a in ("sector", "x", "z", "core"))
    pos = {"sector": y, "x": x, "z": z, "core": core}
    zb = lax.rem(z, 2)
    part = 2 * zb + core
    group = 4 * x + z // 2
    half = lax.rem(x, 2)
    other = 1 - core
    sibling = {**pos, "core": other}
    z_pair = {**pos, "z": z + 1 - 2 * zb}
    x_to = [{**pos, "x": lax.rem(x + dx, NX)} for dx in range(NX)]
    z_to = [{**pos, "z": lax.rem(z + dz, NZ)} for dz in range(NZ)]
    sectors = (core, other)
    waits = []

    def go(copy):
        copy.start()
        waits.append(copy)
        return copy

    part_row = pl.multiple_of(part * COLS, COLS)
    own_left = pltpu.make_async_copy(left, left_v, local_sem.at[0])
    own_wave = pltpu.make_async_copy(wave.at[core], wave_v, local_sem.at[1])
    own_block = pltpu.make_async_copy(
        wave.at[:, pl.ds(part_row, COLS), :], wave_all.at[pl.ds(2 * y, 2)], local_sem.at[2]
    )
    own_block.start()
    own_left.start()
    own_wave.start()

    barrier = pltpu.get_barrier_semaphore()
    partners = (
        [{**pos, "sector": lax.rem(y + k, NY)} for k in (1, NY - 1)] + x_to[1:] + z_to[1:] + [sibling]
    )
    for to in partners:
        pl.semaphore_signal(barrier, inc=1, device_id=to, device_id_type=MESH)
    for term in range(3):
        right_all[part, term] = jnp.concatenate([right[0, term], right[1, term]], axis=1)
    pl.semaphore_wait(barrier, len(partners))

    first = Gather(pos, wave_all, ring_sems[:4])
    send_row = pl.multiple_of(part * COLS + half * HALF, HALF)
    for j in (0, 1):
        first.start(j, wave.at[sectors[j], pl.ds(send_row, HALF), :])
    mine = right_all.at[part]
    go(remote(mine, mine, r_send.at[0], r_recv.at[0], sibling))
    go(remote(mine, mine, r_send.at[1], r_recv.at[1], z_pair))
    first.arrive(1)
    far = right_all.at[2 * (1 - zb) + core]
    remote(far, far, r_send.at[1], r_recv.at[1], z_pair).wait_recv()
    go(remote(far, far, r_send.at[2], r_recv.at[2], sibling))
    first.arrive(2)
    near = right_all.at[2 * zb + other]
    remote(near, near, r_send.at[0], r_recv.at[0], sibling).wait_recv()
    last = right_all.at[2 * (1 - zb) + other]
    remote(last, last, r_send.at[2], r_recv.at[2], sibling).wait_recv()
    low_lanes = lax.broadcasted_iota(jnp.int32, (COLS, 128), 1) < 64
    for term in range(3):
        for a in (0, 1):
            one = right_all[2 * a, term].astype(F32)
            two = right_all[2 * a + 1, term].astype(F32)
            lanes = slice(128 * a, 128 * (a + 1))
            right_full[0, term, :, lanes] = jnp.where(low_lanes, one, pltpu.roll(two, 64, 1)).astype(BF16)
            right_full[1, term, :, lanes] = jnp.where(low_lanes, pltpu.roll(one, 64, 1), two).astype(BF16)
    first.arrive(3)
    first.arrive(4)
    own_left.wait()
    own_wave.wait()
    own_block.wait()
    first.finish()

    for s in (other, core):
        for term in range(3):
            source = shift[3 * group + term, 2 * y + s]
            applied[s, term] = dot(wave_all[source], right_full[s, term]).astype(BF16)
        for q in range(4):
            rows = slice(256 * q, 256 * (q + 1))
            acc = dot(left_v[s, 0, rows, :], applied[s, 0])
            for term in (1, 2):
                acc = acc + dot(left_v[s, term, rows, :], applied[s, term])
            if s is other:
                sib_out[rows, :] = acc.astype(BF16)
                if q % 2 == 1:
                    h = pl.ds(512 * (q // 2), 512)
                    go(remote(sib_out.at[h], sib_in.at[h], sib_send.at[q // 2], sib_recv.at[q // 2], sibling))
            else:
                sigma[rows, :] = acc
    for q in (0, 1):
        h = pl.ds(512 * q, 512)
        remote(sib_out.at[h], sib_in.at[h], sib_send.at[q], sib_recv.at[q], sibling).wait_recv()

    def partial(dx, dz):
        at = 256 * lax.rem(x + dx, NX) + 32 * lax.rem(z + dz, NZ)
        rows = pl.ds(pl.multiple_of(at, 32), 32)
        return sigma[rows, :] + sib_in[rows, :].astype(F32)

    for g in range(4):
        for dx in (2, 1, 3):
            for i in (2 * g, 2 * g + 1):
                x_out[dx - 1, 32 * i : 32 * (i + 1), :] = partial(dx, FAR_FIRST[i]).astype(BF16)
            h = pl.ds(64 * g, 64)
            go(
                remote(
                    x_out.at[dx - 1, h],
                    x_in.at[dx - 1, h],
                    xs_send.at[dx - 1, g],
                    xs_recv.at[dx - 1, g],
                    x_to[dx],
                )
            )
    for i in range(8):
        x_own[32 * i : 32 * (i + 1), :] = partial(0, FAR_FIRST[i])
    for g in range(4):
        rows = slice(64 * g, 64 * (g + 1))
        acc = x_own[rows, :]
        for dx in (1, 2, 3):
            h = pl.ds(64 * g, 64)
            remote(
                x_out.at[dx - 1, h], x_in.at[dx - 1, h], xs_send.at[dx - 1, g], xs_recv.at[dx - 1, g], x_to[dx]
            ).wait_recv()
            acc = acc + x_in[dx - 1, rows, :].astype(F32)
        for i in (2 * g, 2 * g + 1):
            piece = acc[32 * (i % 2) : 32 * (i % 2 + 1), :]
            if FAR_FIRST[i]:
                z_out[i] = piece.astype(BF16)
                go(remote(z_out.at[i], z_in.at[i], zs_send.at[i], zs_recv.at[i], z_to[FAR_FIRST[i]]))
            else:
                z_own[...] = piece
    acc = z_own[...]
    for i in range(7):
        remote(z_out.at[i], z_in.at[i], zs_send.at[i], zs_recv.at[i], z_to[FAR_FIRST[i]]).wait_recv()
        acc = acc + z_in[i].astype(F32)

    def piece_at(dx, dz):
        at = 256 * lax.rem(x + NX - dx, NX) + 32 * lax.rem(z + NZ - dz, NZ)
        return total.at[pl.ds(pl.multiple_of(at, 32), 32)]

    own_piece = piece_at(0, 0)
    own_piece[...] = acc.astype(BF16)
    for i in range(7):
        go(remote(own_piece, own_piece, gz_send.at[i], gz_recv.at[i], z_to[FAR_FIRST[i]]))
    for i in range(7, -1, -1):
        piece = piece_at(0, FAR_FIRST[i])
        if i < 7:
            remote(piece, piece, gz_send.at[i], gz_recv.at[i], z_to[FAR_FIRST[i]]).wait_recv()
        for dx in (2, 1, 3):
            go(remote(piece, piece, gx_send.at[dx - 1, i], gx_recv.at[dx - 1, i], x_to[dx]))
    for i in range(7, -1, -1):
        for dx in (1, 2, 3):
            piece = piece_at(dx, FAR_FIRST[i])
            remote(piece, piece, gx_send.at[dx - 1, i], gx_recv.at[dx - 1, i], x_to[dx]).wait_recv()

    limit = live[2 * y + core]
    gram = jnp.zeros((COLS, COLS), F32)
    cross = jnp.zeros((COLS, COLS), F32)
    for q in range(4):
        rows = slice(256 * q, 256 * (q + 1))
        row_ids = 256 * q + lax.broadcasted_iota(jnp.int32, (256, COLS), 0)
        value = wave_v[rows, :].astype(F32) - STEP_SIZE * total[rows, :].astype(F32)
        high, low = two_parts(jnp.where(row_ids < limit, value, 0.0))
        u_high[rows, :] = high
        u_low[rows, :] = low
        gram = gram + dot_over_rows(high, high)
        cross = cross + dot_over_rows(high, low)
    gram = gram + (cross + cross.T)
    diagonal = lax.broadcasted_iota(jnp.int32, (COLS, COLS), 0) == lax.broadcasted_iota(jnp.int32, (COLS, COLS), 1)
    trace = jnp.sum(jnp.where(diagonal, gram, 0.0), keepdims=True) + EPSILON
    three_halves = jnp.where(diagonal, 1.5, 0.0)
    y0 = gram / trace
    factor = three_halves - 0.5 * y0
    root[...] = dot3(two_parts(y0), two_parts(factor))
    inverse[...] = factor

    def newton_schulz(_, carry):
        y_parts, z_parts = two_parts(root[...]), two_parts(inverse[...])
        f_parts = two_parts(three_halves - 0.5 * dot3(z_parts, y_parts))
        root[...] = dot3(y_parts, f_parts)
        inverse[...] = dot3(f_parts, z_parts)
        return carry

    lax.fori_loop(0, STEPS - 2, newton_schulz, 0)
    y_parts, z_parts = two_parts(root[...]), two_parts(inverse[...])
    f_parts = two_parts(three_halves - 0.5 * dot3(z_parts, y_parts))
    z_parts = two_parts(dot3(f_parts, z_parts))
    scale = jnp.sqrt(ROWS / trace)

    second = Gather(pos, iso_all, ring_sems[4:])
    for h in (0, 1):
        base = pl.multiple_of(512 * (zb if h == 0 else 1 - zb), 512)
        for q in (0, 1):
            rows = pl.ds(base + 256 * q, 256)
            a = (u_high[rows, :], u_low[rows, :])
            iso[core, rows, :] = (dot3(a, z_parts) * scale).astype(BF16)
        block = iso.at[core, pl.ds(base, 512)]
        go(remote(block, block, i_send.at[h], i_recv.at[h], sibling))
        if h == 0:
            second.start(0, iso.at[core, pl.ds(send_row, HALF), :])

    def from_sibling(h):
        base = pl.multiple_of(512 * (zb if h == 0 else 1 - zb), 512)
        block = iso.at[other, pl.ds(base, 512)]
        remote(block, block, i_send.at[h], i_recv.at[h], sibling).wait_recv()

    from_sibling(0)
    second.start(1, iso.at[other, pl.ds(send_row, HALF), :])

    def project(s):
        for term in range(3):
            front[s, term] = dot_over_rows(iso[s], left_v[s, term]).astype(BF16)

    project(core)
    second.arrive(1)
    from_sibling(1)
    project(other)
    second.arrive(2)
    for s in (0, 1):
        iso_all[2 * y + s] = iso[s, pl.ds(part_row, COLS), :]
        iso_out[s] = iso[s, pl.ds(pl.multiple_of(16 * (2 * (NZ * x + z) + core), 16), 16), :]
    second.arrive(3)
    second.arrive(4)
    second.finish()

    for term in range(3):
        values = [
            dot(front[s, term], iso_all[shift[3 * group + term, 2 * y + s]]) * (1 / 32) for s in (0, 1)
        ]
        for a in (0, 1):
            one, two = (v[:, 128 * a : 128 * (a + 1)] for v in values)
            for_zero = jnp.where(low_lanes, one, pltpu.roll(two, 64, 1))
            for_one = jnp.where(low_lanes, pltpu.roll(one, 64, 1), two)
            e_own[a, term] = jnp.where(core == 0, for_zero, for_one)
            e_out[term, a] = jnp.where(core == 0, for_one, for_zero).astype(BF16)
        go(remote(e_out.at[term], e_in.at[term], e_send.at[term], e_recv.at[term], sibling))
    for term in range(3):
        remote(e_out.at[term], e_in.at[term], e_send.at[term], e_recv.at[term], sibling).wait_recv()
        ez_out[term] = (e_own[1 - zb, term] + e_in[term, 1 - zb].astype(F32)).astype(BF16)
        go(remote(ez_out.at[term], ez_in.at[term], ez_send.at[term], ez_recv.at[term], z_pair))
    for term in range(3):
        kept = e_own[zb, term] + e_in[term, zb].astype(F32)
        remote(ez_out.at[term], ez_in.at[term], ez_send.at[term], ez_recv.at[term], z_pair).wait_recv()
        kept = kept + ez_in[term].astype(F32)
        env_out[0, term] = kept[:, :64].astype(BF16)
        env_out[1, term] = pltpu.roll(kept, 64, 1)[:, :64].astype(BF16)

    for copy in waits + first.started + second.started:
        copy.wait_send()


def body(wave_in, left_env, right_env, shift_map, live_rows):
    dma = pltpu.SemaphoreType.DMA
    vmem, smem, anywhere = (pl.BlockSpec(memory_space=m) for m in (pltpu.VMEM, pltpu.SMEM, pl.ANY))
    scratch = [
        pltpu.VMEM((2, 3, ROWS, COLS), BF16),
        pltpu.VMEM((ROWS, COLS), BF16),
        pltpu.VMEM((16, COLS, COLS), BF16),
        pltpu.VMEM((4, 3, COLS, 128), BF16),
        pltpu.VMEM((2, 3, COLS, COLS), BF16),
        pltpu.VMEM((2, 3, COLS, COLS), BF16),
        pltpu.VMEM((ROWS, COLS), BF16),
        pltpu.VMEM((ROWS, COLS), BF16),
        pltpu.VMEM((ROWS, COLS), F32),
        pltpu.VMEM((3, 256, COLS), BF16),
        pltpu.VMEM((256, COLS), F32),
        pltpu.VMEM((3, 256, COLS), BF16),
        pltpu.VMEM((7, 32, COLS), BF16),
        pltpu.VMEM((32, COLS), F32),
        pltpu.VMEM((7, 32, COLS), BF16),
        pltpu.VMEM((ROWS, COLS), BF16),
        pltpu.VMEM((ROWS, COLS), BF16),
        pltpu.VMEM((ROWS, COLS), BF16),
        pltpu.VMEM((COLS, COLS), F32),
        pltpu.VMEM((COLS, COLS), F32),
        pltpu.VMEM((2, ROWS, COLS), BF16),
        pltpu.VMEM((16, COLS, COLS), BF16),
        pltpu.VMEM((2, 3, COLS, COLS), BF16),
        pltpu.VMEM((3, 2, COLS, 128), BF16),
        pltpu.VMEM((3, 2, COLS, 128), BF16),
        pltpu.VMEM((2, 3, COLS, 128), F32),
        pltpu.VMEM((3, COLS, 128), BF16),
        pltpu.VMEM((3, COLS, 128), BF16),
        dma((3,)),
        *[dma((3,))] * 2,
        *[dma((2,))] * 2,
        *[dma((3, 4))] * 2,
        *[dma((7,))] * 2,
        *[dma((7,))] * 2,
        *[dma((3, 8))] * 2,
        *[dma((2,))] * 2,
        *[dma((3,))] * 2,
        *[dma((3,))] * 2,
        *[dma((2, 4, 2))] * 8,
    ]
    return pl.pallas_call(
        kernel,
        out_shape=(
            jax.ShapeDtypeStruct((2, 16, COLS), BF16),
            jax.ShapeDtypeStruct((2, 3, COLS, 64), BF16),
        ),
        in_specs=[smem, smem, anywhere, anywhere, vmem],
        out_specs=(vmem, vmem),
        scratch_shapes=scratch,
        compiler_params=pltpu.CompilerParams(
            collective_id=0, has_side_effects=True, vmem_limit_bytes=40 * 2**20
        ),
        cost_estimate=pl.CostEstimate(flops=8 * 10**9, bytes_accessed=8 * 2**20, transcendentals=0),
        name="dmrg_window",
    )(shift_map, live_rows, wave_in, left_env, right_env)


def solution(mesh):
    split = Mesh(mesh.devices.reshape(NY, NX, NZ, 2), ("sector", *TERM))
    return jax.shard_map(
        body,
        mesh=split,
        in_specs=(
            P("sector", None, None),
            P("sector", TERM, None, None),
            P("sector", TERM, None, None),
            P(),
            P(),
        ),
        out_specs=(P("sector", TERM, None), P("sector", TERM, None, None)),
        check_vma=False,
    )
```

```python
import jax
import jax.numpy as jnp
from jax import lax
from jax.experimental import pallas as pl
from jax.experimental.pallas import tpu as pltpu
from jax.sharding import Mesh
from jax.sharding import PartitionSpec as P

STEPS = 8
NY, NX, NZ = 8, 4, 8
ROWS, COLS, HALF = 1024, 256, 128
TERM = ("x", "z", "core")
STEP_SIZE = 0.15
EPSILON = 1e-06
MESH = pl.DeviceIdType.MESH
F32, BF16 = jnp.float32, jnp.bfloat16
FAR_FIRST = (4, 3, 5, 2, 6, 1, 7, 0)


def dot(a, b):
    return jnp.dot(a, b, preferred_element_type=F32)


def dot_over_rows(a, b):
    return lax.dot_general(a, b, (((0,), (0,)), ((), ())), preferred_element_type=F32)


def dot_over_columns(a, b):
    return lax.dot_general(a, b, (((1,), (1,)), ((), ())), preferred_element_type=F32)


def two_parts(a):
    high = a.astype(BF16)
    return high, (a - high.astype(F32)).astype(BF16)


def dot3(a, b):
    return dot(a[0], b[0]) + (dot(a[0], b[1]) + dot(a[1], b[0]))


def remote(src, dst, send, recv, to):
    return pltpu.make_async_remote_copy(
        src_ref=src, dst_ref=dst, send_sem=send, recv_sem=recv, device_id=to, device_id_type=MESH
    )


class Gather:
    def __init__(self, pos, blocks, sems):
        self.pos, self.blocks = pos, blocks
        self.y_send, self.y_recv, self.x_send, self.x_recv = sems
        self.half = lax.rem(pos["x"], 2)
        self.started = []

    def place(self, way, d, j, half):
        y, core = self.pos["sector"], self.pos["core"]
        step = d if way == 0 else NY - d
        sector = core if j == 0 else 1 - core
        index = 2 * lax.rem(y - step + 2 * NY, NY) + sector
        return self.blocks.at[index, pl.ds(pl.multiple_of(half * HALF, HALF), HALF), :]

    def to_y(self, way):
        y = self.pos["sector"]
        return {**self.pos, "sector": lax.rem(y + (1 if way == 0 else NY - 1), NY)}

    def to_x(self, j):
        x = self.pos["x"]
        return {**self.pos, "x": lax.rem(x + (1 if j == 0 else NX - 1), NX)}

    def go(self, copy):
        copy.start()
        self.started.append(copy)

    def start(self, j, source):
        for way in (0, 1):
            self.go(
                remote(
                    source,
                    self.place(way, 0, j, self.half),
                    self.y_send.at[way, 0, j],
                    self.y_recv.at[way, 0, j],
                    self.to_y(way),
                )
            )

    def arrive(self, d):
        for j in (0, 1):
            for way in (0, 1):
                if d == 4 and j != way:
                    continue
                block = self.place(way, d, j, self.half)
                remote(
                    block,
                    block,
                    self.y_send.at[way, d - 1, j],
                    self.y_recv.at[way, d - 1, j],
                    self.to_y(way),
                ).wait_recv()
                if d < 3 or (d == 3 and j == way):
                    self.go(
                        remote(
                            block,
                            block,
                            self.y_send.at[way, d, j],
                            self.y_recv.at[way, d, j],
                            self.to_y(way),
                        )
                    )
                self.go(
                    remote(
                        block,
                        block,
                        self.x_send.at[way, d - 1, j],
                        self.x_recv.at[way, d - 1, j],
                        self.to_x(j),
                    )
                )

    def finish(self):
        for d in (1, 2, 3, 4):
            for j in (0, 1):
                for way in (0, 1):
                    if d == 4 and j != way:
                        continue
                    block = self.place(way, d, j, 1 - self.half)
                    remote(
                        block,
                        block,
                        self.x_send.at[way, d - 1, j],
                        self.x_recv.at[way, d - 1, j],
                        self.to_x(j),
                    ).wait_recv()


def kernel(
    shift,
    live,
    wave,
    left,
    right,
    iso_out,
    env_out,
    left_v,
    wave_v,
    wave_all,
    right_all,
    applied,
    sib_out,
    sib_in,
    sigma,
    x_out,
    x_own,
    x_in,
    z_out,
    z_own,
    z_in,
    total,
    u_high,
    u_low,
    root,
    inverse,
    iso,
    iso_all,
    front,
    e_out,
    e_in,
    e_own,
    ez_out,
    ez_in,
    local_sem,
    r_send,
    r_recv,
    sib_send,
    sib_recv,
    xs_send,
    xs_recv,
    zs_send,
    zs_recv,
    gz_send,
    gz_recv,
    gx_send,
    gx_recv,
    i_send,
    i_recv,
    e_send,
    e_recv,
    ez_send,
    ez_recv,
    *ring_sems,
):
    y, x, z, core = (lax.axis_index(a) for a in ("sector", "x", "z", "core"))
    pos = {"sector": y, "x": x, "z": z, "core": core}
    zb = lax.rem(z, 2)
    part = 2 * zb + core
    group = 4 * x + z // 2
    half = lax.rem(x, 2)
    other = 1 - core
    sibling = {**pos, "core": other}
    z_pair = {**pos, "z": z + 1 - 2 * zb}
    x_to = [{**pos, "x": lax.rem(x + dx, NX)} for dx in range(NX)]
    z_to = [{**pos, "z": lax.rem(z + dz, NZ)} for dz in range(NZ)]
    sectors = (core, other)
    waits = []

    def go(copy):
        copy.start()
        waits.append(copy)
        return copy

    part_row = pl.multiple_of(part * COLS, COLS)
    own_left = pltpu.make_async_copy(left, left_v, local_sem.at[0])
    own_wave = pltpu.make_async_copy(wave.at[core], wave_v, local_sem.at[1])
    own_block = pltpu.make_async_copy(
        wave.at[:, pl.ds(part_row, COLS), :], wave_all.at[pl.ds(2 * y, 2)], local_sem.at[2]
    )
    own_block.start()
    own_left.start()
    own_wave.start()

    barrier = pltpu.get_barrier_semaphore()
    partners = (
        [{**pos, "sector": lax.rem(y + k, NY)} for k in (1, NY - 1)] + x_to[1:] + z_to[1:] + [sibling]
    )
    for to in partners:
        pl.semaphore_signal(barrier, inc=1, device_id=to, device_id_type=MESH)
    pl.semaphore_wait(barrier, len(partners))

    first = Gather(pos, wave_all, ring_sems[:4])
    send_row = pl.multiple_of(part * COLS + half * HALF, HALF)
    for j in (0, 1):
        first.start(j, wave.at[sectors[j], pl.ds(send_row, HALF), :])
    def right_rows(p):
        return right_all.at[:, :, pl.ds(pl.multiple_of(64 * p, 64), 64), :]

    mine = right_rows(part)
    own_right = pltpu.make_async_copy(right, mine, local_sem.at[3])
    own_right.start()
    go(remote(right, mine, r_send.at[0], r_recv.at[0], sibling))
    go(remote(right, mine, r_send.at[1], r_recv.at[1], z_pair))
    first.arrive(1)
    far = right_rows(2 * (1 - zb) + core)
    remote(far, far, r_send.at[1], r_recv.at[1], z_pair).wait_recv()
    go(remote(far, far, r_send.at[2], r_recv.at[2], sibling))
    first.arrive(2)
    near = right_rows(2 * zb + other)
    remote(near, near, r_send.at[0], r_recv.at[0], sibling).wait_recv()
    last = right_rows(2 * (1 - zb) + other)
    remote(last, last, r_send.at[2], r_recv.at[2], sibling).wait_recv()
    first.arrive(3)
    first.arrive(4)
    own_left.wait()
    own_wave.wait()
    own_block.wait()
    own_right.wait()
    first.finish()

    for s in (other, core):
        for term in range(3):
            source = shift[2 * y + s, 3 * group + term]
            applied[s, term] = dot_over_columns(wave_all[source], right_all[s, term]).astype(BF16)
        for q in range(4):
            rows = slice(256 * q, 256 * (q + 1))
            acc = dot(left_v[s, 0, rows, :], applied[s, 0])
            for term in (1, 2):
                acc = acc + dot(left_v[s, term, rows, :], applied[s, term])
            if s is other:
                sib_out[rows, :] = acc.astype(BF16)
                if q % 2 == 1:
                    h = pl.ds(512 * (q // 2), 512)
                    go(remote(sib_out.at[h], sib_in.at[h], sib_send.at[q // 2], sib_recv.at[q // 2], sibling))
            else:
                sigma[rows, :] = acc
    for q in (0, 1):
        h = pl.ds(512 * q, 512)
        remote(sib_out.at[h], sib_in.at[h], sib_send.at[q], sib_recv.at[q], sibling).wait_recv()

    def partial(dx, dz):
        at = 256 * lax.rem(x + dx, NX) + 32 * lax.rem(z + dz, NZ)
        rows = pl.ds(pl.multiple_of(at, 32), 32)
        return sigma[rows, :] + sib_in[rows, :].astype(F32)

    for g in range(4):
        for dx in (2, 1, 3):
            for i in (2 * g, 2 * g + 1):
                x_out[dx - 1, 32 * i : 32 * (i + 1), :] = partial(dx, FAR_FIRST[i]).astype(BF16)
            h = pl.ds(64 * g, 64)
            go(
                remote(
                    x_out.at[dx - 1, h],
                    x_in.at[dx - 1, h],
                    xs_send.at[dx - 1, g],
                    xs_recv.at[dx - 1, g],
                    x_to[dx],
                )
            )
    for i in range(8):
        x_own[32 * i : 32 * (i + 1), :] = partial(0, FAR_FIRST[i])
    for g in range(4):
        rows = slice(64 * g, 64 * (g + 1))
        acc = x_own[rows, :]
        for dx in (1, 2, 3):
            h = pl.ds(64 * g, 64)
            remote(
                x_out.at[dx - 1, h], x_in.at[dx - 1, h], xs_send.at[dx - 1, g], xs_recv.at[dx - 1, g], x_to[dx]
            ).wait_recv()
            acc = acc + x_in[dx - 1, rows, :].astype(F32)
        for i in (2 * g, 2 * g + 1):
            piece = acc[32 * (i % 2) : 32 * (i % 2 + 1), :]
            if FAR_FIRST[i]:
                z_out[i] = piece.astype(BF16)
                go(remote(z_out.at[i], z_in.at[i], zs_send.at[i], zs_recv.at[i], z_to[FAR_FIRST[i]]))
            else:
                z_own[...] = piece
    acc = z_own[...]
    for i in range(7):
        remote(z_out.at[i], z_in.at[i], zs_send.at[i], zs_recv.at[i], z_to[FAR_FIRST[i]]).wait_recv()
        acc = acc + z_in[i].astype(F32)

    def piece_at(dx, dz):
        at = 256 * lax.rem(x + NX - dx, NX) + 32 * lax.rem(z + NZ - dz, NZ)
        return total.at[pl.ds(pl.multiple_of(at, 32), 32)]

    own_piece = piece_at(0, 0)
    own_piece[...] = acc.astype(BF16)
    for i in range(7):
        go(remote(own_piece, own_piece, gz_send.at[i], gz_recv.at[i], z_to[FAR_FIRST[i]]))
    for i in range(7, -1, -1):
        piece = piece_at(0, FAR_FIRST[i])
        if i < 7:
            remote(piece, piece, gz_send.at[i], gz_recv.at[i], z_to[FAR_FIRST[i]]).wait_recv()
        for dx in (2, 1, 3):
            go(remote(piece, piece, gx_send.at[dx - 1, i], gx_recv.at[dx - 1, i], x_to[dx]))
    for i in range(7, -1, -1):
        for dx in (1, 2, 3):
            piece = piece_at(dx, FAR_FIRST[i])
            remote(piece, piece, gx_send.at[dx - 1, i], gx_recv.at[dx - 1, i], x_to[dx]).wait_recv()

    limit = live[2 * y + core]
    gram = jnp.zeros((COLS, COLS), F32)
    cross = jnp.zeros((COLS, COLS), F32)
    for q in range(4):
        rows = slice(256 * q, 256 * (q + 1))
        row_ids = 256 * q + lax.broadcasted_iota(jnp.int32, (256, COLS), 0)
        value = wave_v[rows, :].astype(F32) - STEP_SIZE * total[rows, :].astype(F32)
        high, low = two_parts(jnp.where(row_ids < limit, value, 0.0))
        u_high[rows, :] = high
        u_low[rows, :] = low
        gram = gram + dot_over_rows(high, high)
        cross = cross + dot_over_rows(high, low)
    gram = gram + (cross + cross.T)
    diagonal = lax.broadcasted_iota(jnp.int32, (COLS, COLS), 0) == lax.broadcasted_iota(jnp.int32, (COLS, COLS), 1)
    trace = jnp.sum(jnp.where(diagonal, gram, 0.0), keepdims=True) + EPSILON
    three_halves = jnp.where(diagonal, 1.5, 0.0)
    y0 = gram / trace
    factor = three_halves - 0.5 * y0
    root[...] = dot3(two_parts(y0), two_parts(factor))
    inverse[...] = factor

    def newton_schulz(_, carry):
        y_parts, z_parts = two_parts(root[...]), two_parts(inverse[...])
        f_parts = two_parts(three_halves - 0.5 * dot3(z_parts, y_parts))
        root[...] = dot3(y_parts, f_parts)
        inverse[...] = dot3(f_parts, z_parts)
        return carry

    lax.fori_loop(0, STEPS - 2, newton_schulz, 0)
    y_parts, z_parts = two_parts(root[...]), two_parts(inverse[...])
    f_parts = two_parts(three_halves - 0.5 * dot3(z_parts, y_parts))
    z_parts = two_parts(dot3(f_parts, z_parts))
    scale = jnp.sqrt(ROWS / trace)

    second = Gather(pos, iso_all, ring_sems[4:])
    for h in (0, 1):
        base = pl.multiple_of(512 * (zb if h == 0 else 1 - zb), 512)
        for q in (0, 1):
            rows = pl.ds(base + 256 * q, 256)
            a = (u_high[rows, :], u_low[rows, :])
            iso[core, rows, :] = (dot3(a, z_parts) * scale).astype(BF16)
        block = iso.at[core, pl.ds(base, 512)]
        go(remote(block, block, i_send.at[h], i_recv.at[h], sibling))
        if h == 0:
            second.start(0, iso.at[core, pl.ds(send_row, HALF), :])

    def from_sibling(h):
        base = pl.multiple_of(512 * (zb if h == 0 else 1 - zb), 512)
        block = iso.at[other, pl.ds(base, 512)]
        remote(block, block, i_send.at[h], i_recv.at[h], sibling).wait_recv()

    from_sibling(0)
    second.start(1, iso.at[other, pl.ds(send_row, HALF), :])

    def project(s):
        for term in range(3):
            front[s, term] = dot_over_rows(left_v[s, term], iso[s]).astype(BF16)

    project(core)
    second.arrive(1)
    from_sibling(1)
    project(other)
    second.arrive(2)
    for s in (0, 1):
        iso_all[2 * y + s] = iso[s, pl.ds(part_row, COLS), :]
        iso_out[s] = iso[s, pl.ds(pl.multiple_of(16 * (2 * (NZ * x + z) + core), 16), 16), :]
    second.arrive(3)
    second.arrive(4)
    second.finish()

    for term in range(3):
        for s in (0, 1):
            source = shift[2 * y + s, 3 * group + term]
            value = dot_over_rows(iso_all[source], front[s, term]) * (1 / 32)
            for a in (0, 1):
                one, two = value[128 * a : 128 * a + 64, :], value[128 * a + 64 : 128 * (a + 1), :]
                e_own[a, term, s] = jnp.where(core == 0, one, two)
                e_out[term, a, s] = jnp.where(core == 0, two, one).astype(BF16)
        go(remote(e_out.at[term], e_in.at[term], e_send.at[term], e_recv.at[term], sibling))
    for term in range(3):
        remote(e_out.at[term], e_in.at[term], e_send.at[term], e_recv.at[term], sibling).wait_recv()
        ez_out[term] = (e_own[1 - zb, term] + e_in[term, 1 - zb].astype(F32)).astype(BF16)
        go(remote(ez_out.at[term], ez_in.at[term], ez_send.at[term], ez_recv.at[term], z_pair))
    for term in range(3):
        kept = e_own[zb, term] + e_in[term, zb].astype(F32)
        remote(ez_out.at[term], ez_in.at[term], ez_send.at[term], ez_recv.at[term], z_pair).wait_recv()
        kept = kept + ez_in[term].astype(F32)
        for s in (0, 1):
            env_out[s, term] = kept[s].astype(BF16)

    for copy in waits + first.started + second.started:
        copy.wait_send()


def body(wave_in, left_env, right_env, shift_map, live_rows):
    dma = pltpu.SemaphoreType.DMA
    vmem, smem, anywhere = (pl.BlockSpec(memory_space=m) for m in (pltpu.VMEM, pltpu.SMEM, pl.ANY))
    scratch = [
        pltpu.VMEM((2, 3, ROWS, COLS), BF16),
        pltpu.VMEM((ROWS, COLS), BF16),
        pltpu.VMEM((16, COLS, COLS), BF16),
        pltpu.VMEM((2, 3, COLS, COLS), BF16),
        pltpu.VMEM((2, 3, COLS, COLS), BF16),
        pltpu.VMEM((ROWS, COLS), BF16),
        pltpu.VMEM((ROWS, COLS), BF16),
        pltpu.VMEM((ROWS, COLS), F32),
        pltpu.VMEM((3, 256, COLS), BF16),
        pltpu.VMEM((256, COLS), F32),
        pltpu.VMEM((3, 256, COLS), BF16),
        pltpu.VMEM((7, 32, COLS), BF16),
        pltpu.VMEM((32, COLS), F32),
        pltpu.VMEM((7, 32, COLS), BF16),
        pltpu.VMEM((ROWS, COLS), BF16),
        pltpu.VMEM((ROWS, COLS), BF16),
        pltpu.VMEM((ROWS, COLS), BF16),
        pltpu.VMEM((COLS, COLS), F32),
        pltpu.VMEM((COLS, COLS), F32),
        pltpu.VMEM((2, ROWS, COLS), BF16),
        pltpu.VMEM((16, COLS, COLS), BF16),
        pltpu.VMEM((2, 3, COLS, COLS), BF16),
        pltpu.VMEM((3, 2, 2, 64, COLS), BF16),
        pltpu.VMEM((3, 2, 2, 64, COLS), BF16),
        pltpu.VMEM((2, 3, 2, 64, COLS), F32),
        pltpu.VMEM((3, 2, 64, COLS), BF16),
        pltpu.VMEM((3, 2, 64, COLS), BF16),
        dma((4,)),
        *[dma((3,))] * 2,
        *[dma((2,))] * 2,
        *[dma((3, 4))] * 2,
        *[dma((7,))] * 2,
        *[dma((7,))] * 2,
        *[dma((3, 8))] * 2,
        *[dma((2,))] * 2,
        *[dma((3,))] * 2,
        *[dma((3,))] * 2,
        *[dma((2, 4, 2))] * 8,
    ]
    iso_rows, env_rows = pl.pallas_call(
        kernel,
        out_shape=(
            jax.ShapeDtypeStruct((2, 16, COLS), BF16),
            jax.ShapeDtypeStruct((2, 3, 64, COLS), BF16),
        ),
        in_specs=[smem, smem, anywhere, anywhere, anywhere],
        out_specs=(vmem, vmem),
        scratch_shapes=scratch,
        compiler_params=pltpu.CompilerParams(
            collective_id=0, has_side_effects=True, vmem_limit_bytes=60 * 2**20
        ),
        cost_estimate=pl.CostEstimate(flops=8 * 10**9, bytes_accessed=8 * 2**20, transcendentals=0),
        name="dmrg_window",
    )(shift_map.T, live_rows, wave_in, left_env, right_env.swapaxes(2, 3))
    return iso_rows, env_rows.swapaxes(2, 3)


def solution(mesh):
    split = Mesh(mesh.devices.reshape(NY, NX, NZ, 2), ("sector", *TERM))
    return jax.shard_map(
        body,
        mesh=split,
        in_specs=(
            P("sector", None, None),
            P("sector", TERM, None, None),
            P("sector", TERM, None, None),
            P(),
            P(),
        ),
        out_specs=(P("sector", TERM, None), P("sector", TERM, None, None)),
        check_vma=False,
    )
```

```python
import jax
import jax.numpy as jnp
from jax import lax
from jax.experimental import pallas as pl
from jax.experimental.pallas import tpu as pltpu
from jax.sharding import Mesh
from jax.sharding import PartitionSpec as P

STEPS = 8
NY, NX, NZ = 8, 4, 8
ROWS, COLS, HALF = 1024, 256, 128
CHUNKS = 2
CHUNK = HALF // CHUNKS
TERM = ("x", "z", "core")
STEP_SIZE = 0.15
EPSILON = 1e-06
MESH = pl.DeviceIdType.MESH
F32, BF16 = jnp.float32, jnp.bfloat16
FAR_FIRST = (4, 3, 5, 2, 6, 1, 7, 0)
X_FAR_FIRST = (2, 1, 3, 0)


def dot(a, b):
    return jnp.dot(a, b, preferred_element_type=F32)


def dot_over_rows(a, b):
    return lax.dot_general(a, b, (((0,), (0,)), ((), ())), preferred_element_type=F32)


def dot_over_columns(a, b):
    return lax.dot_general(a, b, (((1,), (1,)), ((), ())), preferred_element_type=F32)


def two_parts(a):
    high = a.astype(BF16)
    return high, (a - high.astype(F32)).astype(BF16)


def dot3(a, b):
    return dot(a[0], b[0]) + (dot(a[0], b[1]) + dot(a[1], b[0]))


def remote(src, dst, send, recv, to):
    return pltpu.make_async_remote_copy(
        src_ref=src, dst_ref=dst, send_sem=send, recv_sem=recv, device_id=to, device_id_type=MESH
    )


class Gather:
    def __init__(self, pos, blocks, sems):
        self.pos, self.blocks = pos, blocks
        self.y_send, self.y_recv, self.x_send, self.x_recv = sems
        self.half = lax.rem(pos["x"], 2)
        self.started = []

    def place(self, way, d, j, k, half):
        y, core = self.pos["sector"], self.pos["core"]
        step = d if way == 0 else NY - d
        sector = core if j == 0 else 1 - core
        index = 2 * lax.rem(y - step + 2 * NY, NY) + sector
        return self.blocks.at[index, pl.ds(pl.multiple_of(half * HALF + k * CHUNK, CHUNK), CHUNK), :]

    def to(self, way, j):
        y, x = self.pos["sector"], self.pos["x"]
        at = dict(self.pos)
        if way is not None:
            at["sector"] = lax.rem(y + (1 if way == 0 else NY - 1), NY)
        if j is not None:
            at["x"] = lax.rem(x + (1 if j == 0 else NX - 1), NX)
        return at

    def neighbours(self):
        ways, sides = (0, 1, None), (0, 1, None)
        return [self.to(w, j) for w in ways for j in sides if w is not None or j is not None]

    def go(self, copy):
        copy.start()
        self.started.append(copy)

    def along_y(self, source, way, d, j, k):
        at = (way, d, j, k)
        place = self.place(way, d, j, k, self.half)
        source = place if source is None else source
        self.go(remote(source, place, self.y_send.at[at], self.y_recv.at[at], self.to(way, None)))

    def along_x(self, way, d, j, k, ahead=False):
        at = (way, d if ahead else d - 1, j, k)
        block = self.place(way, d, j, k, self.half)
        self.go(remote(block, block, self.x_send.at[at], self.x_recv.at[at], self.to(way if ahead else None, j)))

    def start(self, j, source):
        for k in range(CHUNKS):
            for way in (0, 1):
                self.along_y(source.at[pl.ds(CHUNK * k, CHUNK), :], way, 0, j, k)

    def arrive(self, d):
        for j in (0, 1):
            for k in range(CHUNKS):
                for way in (0, 1):
                    if d == 4 and j != way:
                        continue
                    at = (way, d - 1, j, k)
                    block = self.place(way, d, j, k, self.half)
                    remote(block, block, self.y_send.at[at], self.y_recv.at[at], self.to(way, None)).wait_recv()
                    if d < 3 or (d == 3 and j == way):
                        self.along_y(None, way, d, j, k)
                        if d == 3:
                            self.along_x(way, d, j, k, ahead=True)
                    if d < 4:
                        self.along_x(way, d, j, k)

    def finish(self):
        for d in (1, 2, 3, 4):
            for j in (0, 1):
                for k in range(CHUNKS):
                    for way in (0, 1):
                        if d == 4 and j != way:
                            continue
                        at = (way, d - 1, j, k)
                        block = self.place(way, d, j, k, 1 - self.half)
                        remote(block, block, self.x_send.at[at], self.x_recv.at[at], self.to(None, j)).wait_recv()


def kernel(
    shift_in,
    live_in,
    wave,
    left,
    right,
    iso_out,
    env_out,
    shift,
    live,
    left_v,
    wave_v,
    wave_all,
    right_all,
    applied,
    sib_out,
    sib_in,
    sigma,
    x_out,
    x_own,
    x_in,
    z_out,
    z_own,
    z_in,
    total,
    u_high,
    u_low,
    root,
    inverse,
    iso,
    iso_all,
    front,
    e_out,
    e_in,
    e_own,
    ez_out,
    ez_in,
    env_v,
    local_sem,
    r_send,
    r_recv,
    sib_send,
    sib_recv,
    xs_send,
    xs_recv,
    zs_send,
    zs_recv,
    gz_send,
    gz_recv,
    gx_send,
    gx_recv,
    i_send,
    i_recv,
    e_send,
    e_recv,
    ez_send,
    ez_recv,
    *ring_sems,
):
    y, x, z, core = (lax.axis_index(a) for a in ("sector", "x", "z", "core"))
    pos = {"sector": y, "x": x, "z": z, "core": core}
    zb = lax.rem(z, 2)
    part = 2 * zb + core
    group = 4 * x + z // 2
    half = lax.rem(x, 2)
    other = 1 - core
    sibling = {**pos, "core": other}
    z_pair = {**pos, "z": z + 1 - 2 * zb}
    x_to = [{**pos, "x": lax.rem(x + dx, NX)} for dx in range(NX)]
    z_to = [{**pos, "z": lax.rem(z + dz, NZ)} for dz in range(NZ)]
    sectors = (core, other)
    waits = []

    def go(copy):
        copy.start()
        waits.append(copy)
        return copy

    part_row = pl.multiple_of(part * COLS, COLS)
    own_left = pltpu.make_async_copy(left, left_v, local_sem.at[0])
    own_wave = pltpu.make_async_copy(wave.at[core], wave_v, local_sem.at[1])
    own_block = pltpu.make_async_copy(
        wave.at[:, pl.ds(part_row, COLS), :], wave_all.at[pl.ds(2 * y, 2)], local_sem.at[2]
    )

    own_shift = pltpu.make_async_copy(shift_in, shift, local_sem.at[4])
    own_live = pltpu.make_async_copy(live_in, live, local_sem.at[5])
    first = Gather(pos, wave_all, ring_sems[:4])
    barrier = pltpu.get_barrier_semaphore()
    partners = first.neighbours() + [x_to[2]] + z_to[1:] + [sibling]
    for to in partners:
        pl.semaphore_signal(barrier, inc=1, device_id=to, device_id_type=MESH)
    pl.semaphore_wait(barrier, len(partners))

    send_row = pl.multiple_of(part * COLS + half * HALF, HALF)
    for j in (0, 1):
        first.start(j, wave.at[sectors[j], pl.ds(send_row, HALF), :])

    def right_rows(p):
        return right_all.at[:, :, pl.ds(pl.multiple_of(64 * p, 64), 64), :]

    mine = right_rows(part)
    own_right = pltpu.make_async_copy(right, mine, local_sem.at[3])
    go(remote(right, mine, r_send.at[1], r_recv.at[1], z_pair))
    go(remote(right, mine, r_send.at[0], r_recv.at[0], sibling))
    for copy in (own_shift, own_live, own_block, own_right, own_left, own_wave):
        copy.start()
    first.arrive(1)
    first.arrive(2)
    far = right_rows(2 * (1 - zb) + core)
    remote(far, far, r_send.at[1], r_recv.at[1], z_pair).wait_recv()
    go(remote(far, far, r_send.at[2], r_recv.at[2], sibling))
    first.arrive(3)
    near = right_rows(2 * zb + other)
    remote(near, near, r_send.at[0], r_recv.at[0], sibling).wait_recv()
    last = right_rows(2 * (1 - zb) + other)
    remote(last, last, r_send.at[2], r_recv.at[2], sibling).wait_recv()
    for copy in (own_shift, own_live, own_block, own_right, own_left, own_wave):
        copy.wait()
    first.arrive(4)
    first.finish()

    def row_order(dx):
        base = 256 * lax.rem(x + dx, NX)
        return [pl.ds(pl.multiple_of(base + 32 * lax.rem(z + dz, NZ), 32), 32) for dz in FAR_FIRST]

    def partial_sum(s, dx):
        pieces = row_order(dx)
        acc = jnp.zeros((256, COLS), F32)
        for term in range(3):
            rows = jnp.concatenate([left_v[s, term, p, :] for p in pieces], axis=0)
            acc = acc + dot(rows, applied[s, term])
        return acc

    def apply(s):
        for term in range(3):
            source = shift[2 * y + s, 3 * group + term]
            applied[s, term] = dot_over_columns(wave_all[source], right_all[s, term]).astype(BF16)

    def from_sibling_sum(q):
        h = pl.ds(512 * q, 512)
        return remote(sib_out.at[h], sib_in.at[h], sib_send.at[q], sib_recv.at[q], sibling)

    apply(other)
    for i, dx in enumerate(X_FAR_FIRST):
        sib_out[256 * i : 256 * (i + 1), :] = partial_sum(other, dx).astype(BF16)
        if i % 2 == 1:
            go(from_sibling_sum(i // 2))
    apply(core)
    for i in (0, 1):
        sigma[256 * i : 256 * (i + 1), :] = partial_sum(core, X_FAR_FIRST[i])

    for i, dx in enumerate(X_FAR_FIRST):
        if i % 2 == 0:
            from_sibling_sum(i // 2).wait_recv()
        if i < 2:
            acc = sigma[256 * i : 256 * (i + 1), :]
        else:
            acc = partial_sum(core, dx)
        acc = acc + sib_in[256 * i : 256 * (i + 1), :].astype(F32)
        if dx == 0:
            x_own[...] = acc
            continue
        x_out[dx - 1] = acc.astype(BF16)
        for g in range(4):
            h = pl.ds(64 * g, 64)
            go(
                remote(
                    x_out.at[dx - 1, h],
                    x_in.at[dx - 1, h],
                    xs_send.at[dx - 1, g],
                    xs_recv.at[dx - 1, g],
                    x_to[dx],
                )
            )
    for g in range(4):
        rows = slice(64 * g, 64 * (g + 1))
        acc = x_own[rows, :]
        for dx in (1, 2, 3):
            h = pl.ds(64 * g, 64)
            remote(
                x_out.at[dx - 1, h], x_in.at[dx - 1, h], xs_send.at[dx - 1, g], xs_recv.at[dx - 1, g], x_to[dx]
            ).wait_recv()
            acc = acc + x_in[dx - 1, rows, :].astype(F32)
        for i in (2 * g, 2 * g + 1):
            piece = acc[32 * (i % 2) : 32 * (i % 2 + 1), :]
            if FAR_FIRST[i]:
                z_out[i] = piece.astype(BF16)
                go(remote(z_out.at[i], z_in.at[i], zs_send.at[i], zs_recv.at[i], z_to[FAR_FIRST[i]]))
            else:
                z_own[...] = piece
    acc = z_own[...]
    for i in range(7):
        remote(z_out.at[i], z_in.at[i], zs_send.at[i], zs_recv.at[i], z_to[FAR_FIRST[i]]).wait_recv()
        acc = acc + z_in[i].astype(F32)

    def piece_at(dx, dz):
        at = 256 * lax.rem(x + NX - dx, NX) + 32 * lax.rem(z + NZ - dz, NZ)
        return total.at[pl.ds(pl.multiple_of(at, 32), 32)]

    own_piece = piece_at(0, 0)
    own_piece[...] = acc.astype(BF16)
    for i in range(7):
        go(remote(own_piece, own_piece, gz_send.at[i], gz_recv.at[i], z_to[FAR_FIRST[i]]))
    for i in range(7, -1, -1):
        piece = piece_at(0, FAR_FIRST[i])
        if i < 7:
            remote(piece, piece, gz_send.at[i], gz_recv.at[i], z_to[FAR_FIRST[i]]).wait_recv()
        for dx in (2, 1, 3):
            go(remote(piece, piece, gx_send.at[dx - 1, i], gx_recv.at[dx - 1, i], x_to[dx]))

    limit = live[2 * y + core]
    gram = jnp.zeros((COLS, COLS), F32)
    cross = jnp.zeros((COLS, COLS), F32)
    for dx in (0, 1, 3, 2):
        if dx:
            for i in range(7, -1, -1):
                piece = piece_at(dx, FAR_FIRST[i])
                remote(piece, piece, gx_send.at[dx - 1, i], gx_recv.at[dx - 1, i], x_to[dx]).wait_recv()
        base = pl.multiple_of(256 * lax.rem(x + NX - dx, NX), 256)
        rows = pl.ds(base, 256)
        row_ids = base + lax.broadcasted_iota(jnp.int32, (256, COLS), 0)
        value = wave_v[rows, :].astype(F32) - STEP_SIZE * total[rows, :].astype(F32)
        high, low = two_parts(jnp.where(row_ids < limit, value, 0.0))
        u_high[rows, :] = high
        u_low[rows, :] = low
        gram = gram + dot_over_rows(high, high)
        cross = cross + dot_over_rows(high, low)
    gram = gram + (cross + cross.T)
    diagonal = lax.broadcasted_iota(jnp.int32, (COLS, COLS), 0) == lax.broadcasted_iota(jnp.int32, (COLS, COLS), 1)
    trace = jnp.sum(jnp.where(diagonal, gram, 0.0), keepdims=True) + EPSILON
    three_halves = jnp.where(diagonal, 1.5, 0.0)
    y0 = gram / trace
    factor = three_halves - 0.5 * y0
    root[...] = dot3(two_parts(y0), two_parts(factor))
    inverse[...] = factor

    def newton_schulz(_, carry):
        y_parts, z_parts = two_parts(root[...]), two_parts(inverse[...])
        f_parts = two_parts(three_halves - 0.5 * dot3(z_parts, y_parts))
        root[...] = dot3(y_parts, f_parts)
        inverse[...] = dot3(f_parts, z_parts)
        return carry

    lax.fori_loop(0, STEPS - 2, newton_schulz, 0)
    y_parts, z_parts = two_parts(root[...]), two_parts(inverse[...])
    f_parts = two_parts(three_halves - 0.5 * dot3(z_parts, y_parts))
    z_parts = two_parts(dot3(f_parts, z_parts))
    scale = jnp.sqrt(ROWS / trace)

    second = Gather(pos, iso_all, ring_sems[4:])

    def make_rows(b, c, h):
        rows = pl.ds(pl.multiple_of(512 * b + 256 * c + HALF * h, HALF), HALF)
        a = (u_high[rows, :], u_low[rows, :])
        iso[core, b, c, h] = (dot3(a, z_parts) * scale).astype(BF16)

    def swap(n, s):
        asked = 1 - s
        if n == 0:
            block = iso.at[s, zb, asked, half]
        elif n == 1:
            block = iso.at[s, zb, s, half]
        elif n == 2:
            block = iso.at[s, zb, :, 1 - half]
        else:
            block = iso.at[s, 1 - zb]
        return remote(block, block, i_send.at[n], i_recv.at[n], sibling)

    make_rows(zb, core, half)
    second.start(0, iso.at[core, zb, core, half])
    make_rows(zb, other, half)
    go(swap(0, core))
    for c in (core, other):
        make_rows(zb, c, 1 - half)
    for c in (0, 1):
        for h in (0, 1):
            make_rows(1 - zb, c, h)
    swap(0, other).wait_recv()
    second.start(1, iso.at[other, zb, core, half])
    for n in (1, 2, 3):
        go(swap(n, core))

    def project(s):
        rows = iso[s].reshape(ROWS, COLS)
        for term in range(3):
            front[s, term] = dot_over_rows(left_v[s, term], rows).astype(BF16)

    project(core)
    second.arrive(1)
    for n in (1, 2, 3):
        swap(n, other).wait_recv()
    project(other)
    second.arrive(2)
    own_rows = iso.at[:, x // 2, lax.rem(x, 2), z // 4, pl.ds(pl.multiple_of(32 * lax.rem(z, 4) + 16 * core, 16), 16)]
    out_iso = pltpu.make_async_copy(own_rows, iso_out, local_sem.at[6])
    out_iso.start()
    for s in (0, 1):
        iso_all[2 * y + s] = iso[s, zb, core].reshape(COLS, COLS)
    second.arrive(3)
    second.arrive(4)
    second.finish()

    for term in range(3):
        for s in (0, 1):
            source = shift[2 * y + s, 3 * group + term]
            value = dot_over_rows(iso_all[source], front[s, term]) * (1 / 32)
            for a in (0, 1):
                one, two = value[128 * a : 128 * a + 64, :], value[128 * a + 64 : 128 * (a + 1), :]
                e_own[a, term, s] = jnp.where(core == 0, one, two)
                e_out[term, a, s] = jnp.where(core == 0, two, one).astype(BF16)
        go(remote(e_out.at[term], e_in.at[term], e_send.at[term], e_recv.at[term], sibling))
    for term in range(3):
        remote(e_out.at[term], e_in.at[term], e_send.at[term], e_recv.at[term], sibling).wait_recv()
        ez_out[term] = (e_own[1 - zb, term] + e_in[term, 1 - zb].astype(F32)).astype(BF16)
        go(remote(ez_out.at[term], ez_in.at[term], ez_send.at[term], ez_recv.at[term], z_pair))
    outs = [out_iso]
    for term in range(3):
        kept = e_own[zb, term] + e_in[term, zb].astype(F32)
        remote(ez_out.at[term], ez_in.at[term], ez_send.at[term], ez_recv.at[term], z_pair).wait_recv()
        kept = kept + ez_in[term].astype(F32)
        env_v[term] = kept.astype(BF16)
        out_env = pltpu.make_async_copy(env_v.at[term], env_out.at[:, term], local_sem.at[7 + term])
        out_env.start()
        outs.append(out_env)

    for copy in waits + first.started + second.started:
        copy.wait_send()
    for copy in outs:
        copy.wait()


def body(wave_in, left_env, right_env, shift_map, live_rows):
    dma = pltpu.SemaphoreType.DMA
    anywhere = pl.BlockSpec(memory_space=pl.ANY)
    scratch = [
        pltpu.SMEM((16, 48), jnp.int32),
        pltpu.SMEM((16,), jnp.int32),
        pltpu.VMEM((2, 3, ROWS, COLS), BF16),
        pltpu.VMEM((ROWS, COLS), BF16),
        pltpu.VMEM((16, COLS, COLS), BF16),
        pltpu.VMEM((2, 3, COLS, COLS), BF16),
        pltpu.VMEM((2, 3, COLS, COLS), BF16),
        pltpu.VMEM((ROWS, COLS), BF16),
        pltpu.VMEM((ROWS, COLS), BF16),
        pltpu.VMEM((512, COLS), F32),
        pltpu.VMEM((3, 256, COLS), BF16),
        pltpu.VMEM((256, COLS), F32),
        pltpu.VMEM((3, 256, COLS), BF16),
        pltpu.VMEM((7, 32, COLS), BF16),
        pltpu.VMEM((32, COLS), F32),
        pltpu.VMEM((7, 32, COLS), BF16),
        pltpu.VMEM((ROWS, COLS), BF16),
        pltpu.VMEM((ROWS, COLS), BF16),
        pltpu.VMEM((ROWS, COLS), BF16),
        pltpu.VMEM((COLS, COLS), F32),
        pltpu.VMEM((COLS, COLS), F32),
        pltpu.VMEM((2, 2, 2, 2, HALF, COLS), BF16),
        pltpu.VMEM((16, COLS, COLS), BF16),
        pltpu.VMEM((2, 3, COLS, COLS), BF16),
        pltpu.VMEM((3, 2, 2, 64, COLS), BF16),
        pltpu.VMEM((3, 2, 2, 64, COLS), BF16),
        pltpu.VMEM((2, 3, 2, 64, COLS), F32),
        pltpu.VMEM((3, 2, 64, COLS), BF16),
        pltpu.VMEM((3, 2, 64, COLS), BF16),
        pltpu.VMEM((3, 2, 64, COLS), BF16),
        dma((10,)),
        *[dma((3,))] * 2,
        *[dma((2,))] * 2,
        *[dma((3, 4))] * 2,
        *[dma((7,))] * 2,
        *[dma((7,))] * 2,
        *[dma((3, 8))] * 2,
        *[dma((4,))] * 2,
        *[dma((3,))] * 2,
        *[dma((3,))] * 2,
        *[dma((2, 4, 2, CHUNKS))] * 8,
    ]
    iso_rows, env_rows = pl.pallas_call(
        kernel,
        out_shape=(
            jax.ShapeDtypeStruct((2, 16, COLS), BF16),
            jax.ShapeDtypeStruct((2, 3, 64, COLS), BF16),
        ),
        in_specs=[anywhere] * 5,
        out_specs=(anywhere, anywhere),
        scratch_shapes=scratch,
        compiler_params=pltpu.CompilerParams(
            collective_id=0, has_side_effects=True, vmem_limit_bytes=60 * 2**20
        ),
        cost_estimate=pl.CostEstimate(flops=8 * 10**9, bytes_accessed=8 * 2**20, transcendentals=0),
        name="dmrg_window",
    )(shift_map.T, live_rows, wave_in, left_env, right_env.swapaxes(2, 3))
    return iso_rows, env_rows.swapaxes(2, 3)


def solution(mesh):
    split = Mesh(mesh.devices.reshape(NY, NX, NZ, 2), ("sector", *TERM))
    return jax.shard_map(
        body,
        mesh=split,
        in_specs=(
            P("sector", None, None),
            P("sector", TERM, None, None),
            P("sector", TERM, None, None),
            P(),
            P(),
        ),
        out_specs=(P("sector", TERM, None), P("sector", TERM, None, None)),
        check_vma=False,
    )
```

```python
import jax
import jax.numpy as jnp
from jax import lax
from jax.experimental import pallas as pl
from jax.experimental.pallas import tpu as pltpu
from jax.sharding import Mesh
from jax.sharding import PartitionSpec as P

STEPS = 8
NY, NX, NZ = 8, 4, 8
ROWS, COLS, HALF = 1024, 256, 128
CHUNKS = 2
CHUNK = HALF // CHUNKS
TERM = ("x", "z", "core")
STEP_SIZE = 0.15
EPSILON = 1e-06
MESH = pl.DeviceIdType.MESH
F32, BF16 = jnp.float32, jnp.bfloat16
FAR_FIRST = (4, 3, 5, 2, 6, 1, 7, 0)
X_FAR_FIRST = (2, 1, 3, 0)


def dot(a, b):
    return jnp.dot(a, b, preferred_element_type=F32)


def dot_over_rows(a, b):
    return lax.dot_general(a, b, (((0,), (0,)), ((), ())), preferred_element_type=F32)


def dot_over_columns(a, b):
    return lax.dot_general(a, b, (((1,), (1,)), ((), ())), preferred_element_type=F32)


def two_parts(a):
    high = a.astype(BF16)
    return high, (a - high.astype(F32)).astype(BF16)


def dot3(a, b):
    return dot(a[0], b[0]) + (dot(a[0], b[1]) + dot(a[1], b[0]))


def remote(src, dst, send, recv, to):
    return pltpu.make_async_remote_copy(
        src_ref=src, dst_ref=dst, send_sem=send, recv_sem=recv, device_id=to, device_id_type=MESH
    )


class Gather:
    def __init__(self, pos, chunk_at, sems):
        self.pos, self.chunk_at = pos, chunk_at
        self.y_send, self.y_recv, self.x_send, self.x_recv = sems
        self.half = lax.rem(pos["x"], 2)
        self.started = []

    def place(self, way, d, j, k, half):
        y, core = self.pos["sector"], self.pos["core"]
        step = d if way == 0 else NY - d
        sector = core if j == 0 else 1 - core
        index = 2 * lax.rem(y - step + 2 * NY, NY) + sector
        return self.chunk_at(index, half, k)

    def to(self, way, j):
        y, x = self.pos["sector"], self.pos["x"]
        at = dict(self.pos)
        if way is not None:
            at["sector"] = lax.rem(y + (1 if way == 0 else NY - 1), NY)
        if j is not None:
            at["x"] = lax.rem(x + (1 if j == 0 else NX - 1), NX)
        return at

    def neighbours(self):
        ways, sides = (0, 1, None), (0, 1, None)
        return [self.to(w, j) for w in ways for j in sides if w is not None or j is not None]

    def go(self, copy):
        copy.start()
        self.started.append(copy)

    def along_y(self, source, way, d, j, k):
        at = (way, d, j, k)
        place = self.place(way, d, j, k, self.half)
        source = place if source is None else source
        self.go(remote(source, place, self.y_send.at[at], self.y_recv.at[at], self.to(way, None)))

    def along_x(self, way, d, j, k, ahead=False):
        at = (way, d if ahead else d - 1, j, k)
        block = self.place(way, d, j, k, self.half)
        self.go(remote(block, block, self.x_send.at[at], self.x_recv.at[at], self.to(way if ahead else None, j)))

    def start(self, j, source):
        for k in range(CHUNKS):
            for way in (0, 1):
                self.along_y(source(k), way, 0, j, k)

    def arrive(self, d):
        for j in (0, 1):
            for k in range(CHUNKS):
                for way in (0, 1):
                    if d == 4 and j != way:
                        continue
                    at = (way, d - 1, j, k)
                    block = self.place(way, d, j, k, self.half)
                    remote(block, block, self.y_send.at[at], self.y_recv.at[at], self.to(way, None)).wait_recv()
                    if d < 3 or (d == 3 and j == way):
                        self.along_y(None, way, d, j, k)
                        if d == 3:
                            self.along_x(way, d, j, k, ahead=True)
                    if d < 4:
                        self.along_x(way, d, j, k)

    def finish(self):
        for d in (1, 2, 3, 4):
            for j in (0, 1):
                for k in range(CHUNKS):
                    for way in (0, 1):
                        if d == 4 and j != way:
                            continue
                        at = (way, d - 1, j, k)
                        block = self.place(way, d, j, k, 1 - self.half)
                        remote(block, block, self.x_send.at[at], self.x_recv.at[at], self.to(None, j)).wait_recv()


def kernel(
    shift_in,
    live_in,
    wave,
    left,
    right,
    iso_out,
    env_out,
    shift,
    live,
    left_v,
    wave_v,
    wave_all,
    right_all,
    applied,
    sib_out,
    sib_in,
    sigma,
    x_out,
    x_own,
    x_in,
    z_out,
    z_own,
    z_in,
    far_in,
    total,
    u_high,
    u_low,
    root,
    inverse,
    iso,
    iso_all,
    front,
    e_out,
    e_in,
    e_own,
    env_v,
    local_sem,
    r_send,
    r_recv,
    sib_send,
    sib_recv,
    xs_send,
    xs_recv,
    zs_send,
    zs_recv,
    gz_send,
    gz_recv,
    gx_send,
    gx_recv,
    i_send,
    i_recv,
    e_send,
    e_recv,
    fs_send,
    fs_recv,
    f_send,
    f_recv,
    *ring_sems,
):
    y, x, z, core = (lax.axis_index(a) for a in ("sector", "x", "z", "core"))
    pos = {"sector": y, "x": x, "z": z, "core": core}
    zb = lax.rem(z, 2)
    part = 2 * zb + core
    group = 4 * x + z // 2
    half = lax.rem(x, 2)
    other = 1 - core
    sibling = {**pos, "core": other}
    z_pair = {**pos, "z": z + 1 - 2 * zb}
    x_to = [{**pos, "x": lax.rem(x + dx, NX)} for dx in range(NX)]
    z_to = [{**pos, "z": lax.rem(z + dz, NZ)} for dz in range(NZ)]
    sectors = (core, other)
    waits = []

    def go(copy):
        copy.start()
        waits.append(copy)
        return copy

    part_row = pl.multiple_of(part * COLS, COLS)
    own_left = pltpu.make_async_copy(left, left_v, local_sem.at[0])
    own_wave = pltpu.make_async_copy(wave.at[core], wave_v, local_sem.at[1])
    own_block = pltpu.make_async_copy(
        wave.at[:, pl.ds(part_row, COLS), :], wave_all.at[pl.ds(2 * y, 2)], local_sem.at[2]
    )

    own_shift = pltpu.make_async_copy(shift_in, shift, local_sem.at[4])
    own_live = pltpu.make_async_copy(live_in, live, local_sem.at[5])

    def wave_chunk(index, h, k):
        return wave_all.at[index, pl.ds(pl.multiple_of(h * HALF + k * CHUNK, CHUNK), CHUNK), :]

    first = Gather(pos, wave_chunk, ring_sems[:4])
    barrier = pltpu.get_barrier_semaphore()
    far_to = [{**x_to[dx], "z": z_to[4]["z"]} for dx in range(NX)]
    partners = first.neighbours() + [sibling, x_to[2]] + z_to[1:] + far_to[1:]
    for to in partners:
        pl.semaphore_signal(barrier, inc=1, device_id=to, device_id_type=MESH)
    pl.semaphore_wait(barrier, len(partners))

    send_row = part * COLS + half * HALF
    for j in (0, 1):
        first.start(j, lambda k: wave.at[sectors[j], pl.ds(pl.multiple_of(send_row + CHUNK * k, CHUNK), CHUNK), :])

    def right_rows(p):
        return right_all.at[:, :, pl.ds(pl.multiple_of(64 * p, 64), 64), :]

    mine = right_rows(part)
    own_right = pltpu.make_async_copy(right, mine, local_sem.at[3])
    go(remote(right, mine, r_send.at[1], r_recv.at[1], z_pair))
    go(remote(right, mine, r_send.at[0], r_recv.at[0], sibling))
    for copy in (own_shift, own_live, own_block, own_right, own_left, own_wave):
        copy.start()
    first.arrive(1)
    first.arrive(2)
    far = right_rows(2 * (1 - zb) + core)
    remote(far, far, r_send.at[1], r_recv.at[1], z_pair).wait_recv()
    go(remote(far, far, r_send.at[2], r_recv.at[2], sibling))
    first.arrive(3)
    near = right_rows(2 * zb + other)
    remote(near, near, r_send.at[0], r_recv.at[0], sibling).wait_recv()
    last = right_rows(2 * (1 - zb) + other)
    remote(last, last, r_send.at[2], r_recv.at[2], sibling).wait_recv()
    for copy in (own_shift, own_live, own_block, own_right, own_left, own_wave):
        copy.wait()
    first.arrive(4)
    first.finish()

    def row_order(dx):
        base = 256 * lax.rem(x + dx, NX)
        return [pl.ds(pl.multiple_of(base + 32 * lax.rem(z + dz, NZ), 32), 32) for dz in FAR_FIRST]

    def partial_sum(s, dx):
        pieces = row_order(dx)
        acc = jnp.zeros((256, COLS), F32)
        for term in range(3):
            rows = jnp.concatenate([left_v[s, term, p, :] for p in pieces], axis=0)
            acc = acc + dot(rows, applied[s, term])
        return acc

    def apply(s):
        for term in range(3):
            source = shift[2 * y + s, 3 * group + term]
            applied[s, term] = dot_over_columns(wave_all[source], right_all[s, term]).astype(BF16)

    def from_sibling_sum(q):
        h = pl.ds(512 * q, 512)
        return remote(sib_out.at[h], sib_in.at[h], sib_send.at[q], sib_recv.at[q], sibling)

    apply(other)
    for i, dx in enumerate(X_FAR_FIRST):
        sib_out[256 * i : 256 * (i + 1), :] = partial_sum(other, dx).astype(BF16)
        if i % 2 == 1:
            go(from_sibling_sum(i // 2))
    apply(core)
    for i in (0, 1):
        sigma[256 * i : 256 * (i + 1), :] = partial_sum(core, X_FAR_FIRST[i])

    def to_far(dx):
        return remote(
            x_out.at[dx - 1, pl.ds(0, 32)], far_in.at[dx - 1], fs_send.at[dx - 1], fs_recv.at[dx - 1], far_to[dx]
        )

    def to_x(dx, g):
        h = pl.ds(32, 32) if g == 0 else pl.ds(64 * g, 64)
        return remote(
            x_out.at[dx - 1, h], x_in.at[dx - 1, h], xs_send.at[dx - 1, g], xs_recv.at[dx - 1, g], x_to[dx]
        )

    for i, dx in enumerate(X_FAR_FIRST):
        if i % 2 == 0:
            from_sibling_sum(i // 2).wait_recv()
        if i < 2:
            acc = sigma[256 * i : 256 * (i + 1), :]
        else:
            acc = partial_sum(core, dx)
        acc = acc + sib_in[256 * i : 256 * (i + 1), :].astype(F32)
        if dx == 0:
            x_own[...] = acc
            z_out[0] = acc[:32, :].astype(BF16)
            go(remote(z_out.at[0], z_in.at[0], zs_send.at[0], zs_recv.at[0], z_to[4]))
            continue
        x_out[dx - 1] = acc.astype(BF16)
        go(to_far(dx))
        for g in range(4):
            go(to_x(dx, g))
    for g in range(4):
        slots = range(max(1, 2 * g), 2 * g + 2)
        rows = slice(32 * slots[0], 64 * (g + 1))
        acc = x_own[rows, :]
        for dx in (1, 2, 3):
            to_x(dx, g).wait_recv()
            acc = acc + x_in[dx - 1, rows, :].astype(F32)
        for i in slots:
            piece = acc[32 * (i - slots[0]) : 32 * (i - slots[0] + 1), :]
            if FAR_FIRST[i]:
                z_out[i] = piece.astype(BF16)
                go(remote(z_out.at[i], z_in.at[i], zs_send.at[i], zs_recv.at[i], z_to[FAR_FIRST[i]]))
            else:
                z_own[...] = piece
    acc = z_own[...]
    for i in range(7):
        remote(z_out.at[i], z_in.at[i], zs_send.at[i], zs_recv.at[i], z_to[FAR_FIRST[i]]).wait_recv()
        acc = acc + z_in[i].astype(F32)
    for dx in (1, 2, 3):
        to_far(dx).wait_recv()
        acc = acc + far_in[dx - 1].astype(F32)

    def piece_at(dx, dz):
        at = 256 * lax.rem(x + NX - dx, NX) + 32 * lax.rem(z + NZ - dz, NZ)
        return total.at[pl.ds(pl.multiple_of(at, 32), 32)]

    own_piece = piece_at(0, 0)
    own_piece[...] = acc.astype(BF16)
    for i in range(7):
        go(remote(own_piece, own_piece, gz_send.at[i], gz_recv.at[i], z_to[FAR_FIRST[i]]))
        if i == 0:
            for dx in (2, 1, 3):
                go(remote(own_piece, own_piece, gx_send.at[dx - 1, 0], gx_recv.at[dx - 1, 0], far_to[dx]))
    for i in range(7, -1, -1):
        piece = piece_at(0, FAR_FIRST[i])
        if i < 7:
            remote(piece, piece, gz_send.at[i], gz_recv.at[i], z_to[FAR_FIRST[i]]).wait_recv()
        if i == 0:
            continue
        for dx in (2, 1, 3):
            go(remote(piece, piece, gx_send.at[dx - 1, i], gx_recv.at[dx - 1, i], x_to[dx]))

    limit = live[2 * y + core]
    gram = jnp.zeros((COLS, COLS), F32)
    cross = jnp.zeros((COLS, COLS), F32)
    for dx in (0, 1, 3, 2):
        if dx:
            for i in range(7, -1, -1):
                piece = piece_at(dx, FAR_FIRST[i])
                remote(piece, piece, gx_send.at[dx - 1, i], gx_recv.at[dx - 1, i], x_to[dx]).wait_recv()
        base = pl.multiple_of(256 * lax.rem(x + NX - dx, NX), 256)
        rows = pl.ds(base, 256)
        row_ids = base + lax.broadcasted_iota(jnp.int32, (256, COLS), 0)
        value = wave_v[rows, :].astype(F32) - STEP_SIZE * total[rows, :].astype(F32)
        high, low = two_parts(jnp.where(row_ids < limit, value, 0.0))
        u_high[rows, :] = high
        u_low[rows, :] = low
        gram = gram + dot_over_rows(high, high)
        cross = cross + dot_over_rows(high, low)
    gram = gram + (cross + cross.T)
    diagonal = lax.broadcasted_iota(jnp.int32, (COLS, COLS), 0) == lax.broadcasted_iota(jnp.int32, (COLS, COLS), 1)
    trace = jnp.sum(jnp.where(diagonal, gram, 0.0), keepdims=True) + EPSILON
    three_halves = jnp.where(diagonal, 1.5, 0.0)
    y0 = gram / trace
    factor = three_halves - 0.5 * y0
    root[...] = dot3(two_parts(y0), two_parts(factor))
    inverse[...] = factor

    def newton_schulz(_, carry):
        y_parts, z_parts = two_parts(root[...]), two_parts(inverse[...])
        f_parts = two_parts(three_halves - 0.5 * dot3(z_parts, y_parts))
        root[...] = dot3(y_parts, f_parts)
        inverse[...] = dot3(f_parts, z_parts)
        return carry

    lax.fori_loop(0, STEPS - 2, newton_schulz, 0)
    y_parts, z_parts = two_parts(root[...]), two_parts(inverse[...])
    f_parts = two_parts(three_halves - 0.5 * dot3(z_parts, y_parts))
    z_parts = two_parts(dot3(f_parts, z_parts))
    scale = jnp.sqrt(ROWS / trace)

    columns = pl.ds(pl.multiple_of(128 * zb, 128), 128)
    second = Gather(pos, lambda index, h, k: iso_all.at[index, h, k], ring_sems[4:])

    def make_rows(b, c):
        for h in (0, 1):
            rows = pl.ds(pl.multiple_of(512 * b + 256 * c + HALF * h, HALF), HALF)
            a = (u_high[rows, :], u_low[rows, :])
            iso[core, b, c, h] = (dot3(a, z_parts) * scale).astype(BF16)

    def swap(n, s):
        block = (iso.at[s, half, 1 - s], iso.at[s, half, s], iso.at[s, 1 - half])[n]
        return remote(block, block, i_send.at[n], i_recv.at[n], sibling)

    make_rows(half, core)
    second.start(0, lambda k: iso.at[core, half, core, k, :, columns])
    make_rows(half, other)
    go(swap(0, core))
    for c in (0, 1):
        make_rows(1 - half, c)
    go(swap(1, core))
    go(swap(2, core))
    swap(0, other).wait_recv()
    second.start(1, lambda k: iso.at[other, half, core, k, :, columns])

    def to_pair(n, term):
        block = front.at[sectors[n], term, zb]
        return remote(block, block, f_send.at[n, term], f_recv.at[n, term], z_pair)

    def project(n):
        rows = iso[sectors[n]].reshape(ROWS, COLS)
        for term in range(3):
            front[sectors[n], term, zb] = dot_over_rows(left_v[sectors[n], term], rows).astype(BF16)
            go(to_pair(n, term))

    project(0)
    second.arrive(1)
    for n in (1, 2):
        swap(n, other).wait_recv()
    project(1)
    second.arrive(2)
    own_rows = iso.at[:, x // 2, lax.rem(x, 2), z // 4, pl.ds(pl.multiple_of(32 * lax.rem(z, 4) + 16 * core, 16), 16)]
    out_iso = pltpu.make_async_copy(own_rows, iso_out, local_sem.at[6])
    own_block = pltpu.make_async_copy(
        iso.at[:, :, core, :, :, columns], iso_all.at[pl.ds(2 * y, 2)], local_sem.at[7]
    )
    out_iso.start()
    own_block.start()
    second.arrive(3)
    second.arrive(4)
    second.finish()
    own_block.wait()

    def to_sibling(n):
        s = sectors[n]
        return remote(e_out.at[s], e_in.at[s], e_send.at[n], e_recv.at[n], sibling)

    for n, s in enumerate(sectors):
        for term in range(3):
            to_pair(n, term).wait_recv()
            source = shift[2 * y + s, 3 * group + term]
            rows = iso_all[source].reshape(512, 128)
            value = dot_over_rows(rows, front[s, term].reshape(512, COLS)) * (1 / 32)
            e_own[s, term] = jnp.where(core == 0, value[:64, :], value[64:, :])
            e_out[s, term] = jnp.where(core == 0, value[64:, :], value[:64, :]).astype(BF16)
        go(to_sibling(n))
    outs = [out_iso]
    for n in (0, 1):
        s = sectors[1 - n]
        remote(e_out.at[s], e_in.at[s], e_send.at[n], e_recv.at[n], sibling).wait_recv()
        env_v[s] = (e_own[s] + e_in[s].astype(F32)).astype(BF16)
        out_env = pltpu.make_async_copy(env_v.at[s], env_out.at[s], local_sem.at[8 + n])
        out_env.start()
        outs.append(out_env)

    for copy in waits + first.started + second.started:
        copy.wait_send()
    for copy in outs:
        copy.wait()


def body(wave_in, left_env, right_env, shift_map, live_rows):
    dma = pltpu.SemaphoreType.DMA
    anywhere = pl.BlockSpec(memory_space=pl.ANY)
    scratch = [
        pltpu.SMEM((16, 48), jnp.int32),
        pltpu.SMEM((16,), jnp.int32),
        pltpu.VMEM((2, 3, ROWS, COLS), BF16),
        pltpu.VMEM((ROWS, COLS), BF16),
        pltpu.VMEM((16, COLS, COLS), BF16),
        pltpu.VMEM((2, 3, COLS, COLS), BF16),
        pltpu.VMEM((2, 3, COLS, COLS), BF16),
        pltpu.VMEM((ROWS, COLS), BF16),
        pltpu.VMEM((ROWS, COLS), BF16),
        pltpu.VMEM((512, COLS), F32),
        pltpu.VMEM((3, 256, COLS), BF16),
        pltpu.VMEM((256, COLS), F32),
        pltpu.VMEM((3, 256, COLS), BF16),
        pltpu.VMEM((7, 32, COLS), BF16),
        pltpu.VMEM((32, COLS), F32),
        pltpu.VMEM((7, 32, COLS), BF16),
        pltpu.VMEM((3, 32, COLS), BF16),
        pltpu.VMEM((ROWS, COLS), BF16),
        pltpu.VMEM((ROWS, COLS), BF16),
        pltpu.VMEM((ROWS, COLS), BF16),
        pltpu.VMEM((COLS, COLS), F32),
        pltpu.VMEM((COLS, COLS), F32),
        pltpu.VMEM((2, 2, 2, 2, HALF, COLS), BF16),
        pltpu.VMEM((16, 2, 2, HALF, 128), BF16),
        pltpu.VMEM((2, 3, 2, COLS, COLS), BF16),
        pltpu.VMEM((2, 3, 64, COLS), BF16),
        pltpu.VMEM((2, 3, 64, COLS), BF16),
        pltpu.VMEM((2, 3, 64, COLS), F32),
        pltpu.VMEM((2, 3, 64, COLS), BF16),
        dma((10,)),
        *[dma((3,))] * 2,
        *[dma((2,))] * 2,
        *[dma((3, 4))] * 2,
        *[dma((7,))] * 2,
        *[dma((7,))] * 2,
        *[dma((3, 8))] * 2,
        *[dma((3,))] * 2,
        *[dma((2,))] * 2,
        *[dma((3,))] * 2,
        *[dma((2, 3))] * 2,
        *[dma((2, 4, 2, CHUNKS))] * 8,
    ]
    iso_rows, env_rows = pl.pallas_call(
        kernel,
        out_shape=(
            jax.ShapeDtypeStruct((2, 16, COLS), BF16),
            jax.ShapeDtypeStruct((2, 3, 64, COLS), BF16),
        ),
        in_specs=[anywhere] * 5,
        out_specs=(anywhere, anywhere),
        scratch_shapes=scratch,
        compiler_params=pltpu.CompilerParams(
            collective_id=0, has_side_effects=True, vmem_limit_bytes=60 * 2**20
        ),
        cost_estimate=pl.CostEstimate(flops=8 * 10**9, bytes_accessed=8 * 2**20, transcendentals=0),
        name="dmrg_window",
    )(shift_map.T, live_rows, wave_in, left_env, right_env.swapaxes(2, 3))
    return iso_rows, env_rows.swapaxes(2, 3)


def solution(mesh):
    split = Mesh(mesh.devices.reshape(NY, NX, NZ, 2), ("sector", *TERM))
    return jax.shard_map(
        body,
        mesh=split,
        in_specs=(
            P("sector", None, None),
            P("sector", TERM, None, None),
            P("sector", TERM, None, None),
            P(),
            P(),
        ),
        out_specs=(P("sector", TERM, None), P("sector", TERM, None, None)),
        check_vma=False,
    )
```

```python
import jax
import jax.numpy as jnp
from jax import lax
from jax.experimental import pallas as pl
from jax.experimental.pallas import tpu as pltpu
from jax.sharding import Mesh
from jax.sharding import PartitionSpec as P

STEPS = 8
NY, NX, NZ = 8, 4, 8
ROWS, COLS, HALF = 1024, 256, 128
CHUNKS = 2
CHUNK = HALF // CHUNKS
TERM = ("x", "z", "core")
STEP_SIZE = 0.15
EPSILON = 1e-06
MESH = pl.DeviceIdType.MESH
F32, BF16 = jnp.float32, jnp.bfloat16
FAR_FIRST = (4, 3, 5, 2, 6, 1, 7, 0)
X_FAR_FIRST = (2, 1, 3, 0)


def dot(a, b):
    return jnp.dot(a, b, preferred_element_type=F32)


def dot_over_rows(a, b):
    return lax.dot_general(a, b, (((0,), (0,)), ((), ())), preferred_element_type=F32)


def dot_over_columns(a, b):
    return lax.dot_general(a, b, (((1,), (1,)), ((), ())), preferred_element_type=F32)


def two_parts(a):
    high = a.astype(BF16)
    return high, (a - high.astype(F32)).astype(BF16)


def dot3(a, b):
    return dot(a[0], b[0]) + (dot(a[0], b[1]) + dot(a[1], b[0]))


def remote(src, dst, send, recv, to):
    return pltpu.make_async_remote_copy(
        src_ref=src, dst_ref=dst, send_sem=send, recv_sem=recv, device_id=to, device_id_type=MESH
    )


class Gather:
    def __init__(self, pos, chunk_at, sems):
        self.pos, self.chunk_at = pos, chunk_at
        self.y_send, self.y_recv, self.x_send, self.x_recv = sems
        self.half = lax.rem(pos["x"], 2)
        self.started = []

    def place(self, way, d, j, k, half):
        y, core = self.pos["sector"], self.pos["core"]
        step = d if way == 0 else NY - d
        sector = core if j == 0 else 1 - core
        index = 2 * lax.rem(y - step + 2 * NY, NY) + sector
        return self.chunk_at(index, half, k)

    def to(self, way, j):
        y, x = self.pos["sector"], self.pos["x"]
        at = dict(self.pos)
        if way is not None:
            at["sector"] = lax.rem(y + (1 if way == 0 else NY - 1), NY)
        if j is not None:
            at["x"] = lax.rem(x + (1 if j == 0 else NX - 1), NX)
        return at

    def neighbours(self):
        ways, sides = (0, 1, None), (0, 1, None)
        return [self.to(w, j) for w in ways for j in sides if w is not None or j is not None]

    def go(self, copy):
        copy.start()
        self.started.append(copy)

    def along_y(self, source, way, d, j, k):
        at = (way, d, j, k)
        place = self.place(way, d, j, k, self.half)
        source = place if source is None else source
        self.go(remote(source, place, self.y_send.at[at], self.y_recv.at[at], self.to(way, None)))

    def along_x(self, way, d, j, k, ahead=False):
        at = (way, d if ahead else d - 1, j, k)
        block = self.place(way, d, j, k, self.half)
        self.go(remote(block, block, self.x_send.at[at], self.x_recv.at[at], self.to(way if ahead else None, j)))

    def start(self, j, source):
        for k in range(CHUNKS):
            for way in (0, 1):
                self.along_y(source(k), way, 0, j, k)

    def arrive(self, d):
        for j in (0, 1):
            for k in range(CHUNKS):
                for way in (0, 1):
                    if d == 4 and j != way:
                        continue
                    at = (way, d - 1, j, k)
                    block = self.place(way, d, j, k, self.half)
                    remote(block, block, self.y_send.at[at], self.y_recv.at[at], self.to(way, None)).wait_recv()
                    if d < 3 or (d == 3 and j == way):
                        self.along_y(None, way, d, j, k)
                        if d == 3:
                            self.along_x(way, d, j, k, ahead=True)
                    if d < 4:
                        self.along_x(way, d, j, k)

    def finish(self):
        for d in (1, 2, 3, 4):
            for j in (0, 1):
                for k in range(CHUNKS):
                    for way in (0, 1):
                        if d == 4 and j != way:
                            continue
                        at = (way, d - 1, j, k)
                        block = self.place(way, d, j, k, 1 - self.half)
                        remote(block, block, self.x_send.at[at], self.x_recv.at[at], self.to(None, j)).wait_recv()


def kernel(
    shift_in,
    live_in,
    wave,
    left,
    right,
    iso_out,
    env_out,
    shift,
    live,
    left_v,
    wave_v,
    wave_all,
    right_all,
    applied,
    sib_out,
    sib_in,
    sigma,
    x_out,
    x_own,
    x_in,
    z_out,
    z_own,
    z_in,
    left_pair,
    total,
    u_high,
    u_low,
    root,
    inverse,
    iso,
    iso_all,
    front,
    e_out,
    e_in,
    e_own,
    env_v,
    local_sem,
    r_send,
    r_recv,
    sib_send,
    sib_recv,
    xs_send,
    xs_recv,
    zs_send,
    zs_recv,
    gz_send,
    gz_recv,
    gx_send,
    gx_recv,
    i_send,
    i_recv,
    e_send,
    e_recv,
    l_send,
    l_recv,
    f_send,
    f_recv,
    *ring_sems,
):
    y, x, z, core = (lax.axis_index(a) for a in ("sector", "x", "z", "core"))
    pos = {"sector": y, "x": x, "z": z, "core": core}
    zb = lax.rem(z, 2)
    part = 2 * zb + core
    group = 4 * x + z // 2
    half = lax.rem(x, 2)
    other = 1 - core
    sibling = {**pos, "core": other}
    z_pair = {**pos, "z": z + 1 - 2 * zb}
    x_to = [{**pos, "x": lax.rem(x + dx, NX)} for dx in range(NX)]
    z_to = [{**pos, "z": lax.rem(z + dz, NZ)} for dz in range(NZ)]
    sectors = (core, other)
    waits = []

    def go(copy):
        copy.start()
        waits.append(copy)
        return copy

    part_row = pl.multiple_of(part * COLS, COLS)
    own_left = pltpu.make_async_copy(left, left_v, local_sem.at[0])
    own_wave = pltpu.make_async_copy(wave.at[core], wave_v, local_sem.at[1])
    own_block = pltpu.make_async_copy(
        wave.at[:, pl.ds(part_row, COLS), :], wave_all.at[pl.ds(2 * y, 2)], local_sem.at[2]
    )

    own_shift = pltpu.make_async_copy(shift_in, shift, local_sem.at[4])
    own_live = pltpu.make_async_copy(live_in, live, local_sem.at[5])

    def wave_chunk(index, h, k):
        return wave_all.at[index, pl.ds(pl.multiple_of(h * HALF + k * CHUNK, CHUNK), CHUNK), :]

    first = Gather(pos, wave_chunk, ring_sems[:4])
    barrier = pltpu.get_barrier_semaphore()
    partners = first.neighbours() + [sibling, x_to[2]] + z_to[1:]
    for to in partners:
        pl.semaphore_signal(barrier, inc=1, device_id=to, device_id_type=MESH)
    pl.semaphore_wait(barrier, len(partners))

    send_row = part * COLS + half * HALF
    for j in (0, 1):
        first.start(j, lambda k: wave.at[sectors[j], pl.ds(pl.multiple_of(send_row + CHUNK * k, CHUNK), CHUNK), :])

    def right_rows(p):
        return right_all.at[:, :, pl.ds(pl.multiple_of(64 * p, 64), 64), :]

    mine = right_rows(part)
    own_right = pltpu.make_async_copy(right, mine, local_sem.at[3])
    go(remote(right, mine, r_send.at[1], r_recv.at[1], z_pair))
    go(remote(right, mine, r_send.at[0], r_recv.at[0], sibling))
    for copy in (own_shift, own_live, own_block, own_right, own_left, own_wave):
        copy.start()
    first.arrive(1)
    pair_blocks = remote(left.at[other, pl.ds(1, 2)], left_pair, l_send.at[0], l_recv.at[0], z_pair)
    go(pair_blocks)
    first.arrive(2)
    far = right_rows(2 * (1 - zb) + core)
    remote(far, far, r_send.at[1], r_recv.at[1], z_pair).wait_recv()
    go(remote(far, far, r_send.at[2], r_recv.at[2], sibling))
    first.arrive(3)
    near = right_rows(2 * zb + other)
    remote(near, near, r_send.at[0], r_recv.at[0], sibling).wait_recv()
    last = right_rows(2 * (1 - zb) + other)
    remote(last, last, r_send.at[2], r_recv.at[2], sibling).wait_recv()
    for copy in (own_shift, own_live, own_block, own_right, own_left, own_wave):
        copy.wait()
    first.arrive(4)
    first.finish()

    def row_order(dx):
        base = 256 * lax.rem(x + dx, NX)
        return [pl.ds(pl.multiple_of(base + 32 * lax.rem(z + dz, NZ), 32), 32) for dz in FAR_FIRST]

    def partial_sum(s, dx):
        pieces = row_order(dx)
        acc = jnp.zeros((256, COLS), F32)
        for term in range(3):
            rows = jnp.concatenate([left_v[s, term, p, :] for p in pieces], axis=0)
            acc = acc + dot(rows, applied[s, term])
        return acc

    def apply(s):
        for term in range(3):
            source = shift[2 * y + s, 3 * group + term]
            applied[s, term] = dot_over_columns(wave_all[source], right_all[s, term]).astype(BF16)

    def from_sibling_sum(q):
        h = pl.ds(512 * q, 512)
        return remote(sib_out.at[h], sib_in.at[h], sib_send.at[q], sib_recv.at[q], sibling)

    apply(other)
    for i, dx in enumerate(X_FAR_FIRST):
        sib_out[256 * i : 256 * (i + 1), :] = partial_sum(other, dx).astype(BF16)
        if i % 2 == 1:
            go(from_sibling_sum(i // 2))
    apply(core)
    for i in (0, 1):
        sigma[256 * i : 256 * (i + 1), :] = partial_sum(core, X_FAR_FIRST[i])

    def to_x(dx, g):
        h = pl.ds(64 * g, 64)
        return remote(
            x_out.at[dx - 1, h], x_in.at[dx - 1, h], xs_send.at[dx - 1, g], xs_recv.at[dx - 1, g], x_to[dx]
        )

    for i, dx in enumerate(X_FAR_FIRST):
        if i % 2 == 0:
            from_sibling_sum(i // 2).wait_recv()
        if i < 2:
            acc = sigma[256 * i : 256 * (i + 1), :]
        else:
            acc = partial_sum(core, dx)
        acc = acc + sib_in[256 * i : 256 * (i + 1), :].astype(F32)
        if dx == 0:
            x_own[...] = acc
            continue
        x_out[dx - 1] = acc.astype(BF16)
        for g in range(4):
            go(to_x(dx, g))
    for g in range(4):
        slots = (2 * g, 2 * g + 1)
        rows = slice(64 * g, 64 * (g + 1))
        acc = x_own[rows, :]
        for dx in (1, 2, 3):
            to_x(dx, g).wait_recv()
            acc = acc + x_in[dx - 1, rows, :].astype(F32)
        for i in slots:
            piece = acc[32 * (i - slots[0]) : 32 * (i - slots[0] + 1), :]
            if FAR_FIRST[i]:
                z_out[i] = piece.astype(BF16)
                go(remote(z_out.at[i], z_in.at[i], zs_send.at[i], zs_recv.at[i], z_to[FAR_FIRST[i]]))
            else:
                z_own[...] = piece
    acc = z_own[...]
    for i in range(7):
        remote(z_out.at[i], z_in.at[i], zs_send.at[i], zs_recv.at[i], z_to[FAR_FIRST[i]]).wait_recv()
        acc = acc + z_in[i].astype(F32)

    def piece_at(dx, dz):
        at = 256 * lax.rem(x + NX - dx, NX) + 32 * lax.rem(z + NZ - dz, NZ)
        return total.at[pl.ds(pl.multiple_of(at, 32), 32)]

    own_piece = piece_at(0, 0)
    own_piece[...] = acc.astype(BF16)
    for i in range(7):
        go(remote(own_piece, own_piece, gz_send.at[i], gz_recv.at[i], z_to[FAR_FIRST[i]]))
    for i in range(7, -1, -1):
        piece = piece_at(0, FAR_FIRST[i])
        if i < 7:
            remote(piece, piece, gz_send.at[i], gz_recv.at[i], z_to[FAR_FIRST[i]]).wait_recv()
        for dx in (2, 1, 3):
            go(remote(piece, piece, gx_send.at[dx - 1, i], gx_recv.at[dx - 1, i], x_to[dx]))

    limit = live[2 * y + core]
    gram = jnp.zeros((COLS, COLS), F32)
    cross = jnp.zeros((COLS, COLS), F32)
    for dx in (0, 1, 3, 2):
        if dx:
            for i in range(7, -1, -1):
                piece = piece_at(dx, FAR_FIRST[i])
                remote(piece, piece, gx_send.at[dx - 1, i], gx_recv.at[dx - 1, i], x_to[dx]).wait_recv()
        base = pl.multiple_of(256 * lax.rem(x + NX - dx, NX), 256)
        rows = pl.ds(base, 256)
        row_ids = base + lax.broadcasted_iota(jnp.int32, (256, COLS), 0)
        value = wave_v[rows, :].astype(F32) - STEP_SIZE * total[rows, :].astype(F32)
        high, low = two_parts(jnp.where(row_ids < limit, value, 0.0))
        u_high[rows, :] = high
        u_low[rows, :] = low
        gram = gram + dot_over_rows(high, high)
        cross = cross + dot_over_rows(high, low)
    gram = gram + (cross + cross.T)
    diagonal = lax.broadcasted_iota(jnp.int32, (COLS, COLS), 0) == lax.broadcasted_iota(jnp.int32, (COLS, COLS), 1)
    trace = jnp.sum(jnp.where(diagonal, gram, 0.0), keepdims=True) + EPSILON
    three_halves = jnp.where(diagonal, 1.5, 0.0)
    y0 = gram / trace
    factor = three_halves - 0.5 * y0
    root[...] = dot3(two_parts(y0), two_parts(factor))
    inverse[...] = factor

    def newton_schulz(_, carry):
        y_parts, z_parts = two_parts(root[...]), two_parts(inverse[...])
        f_parts = two_parts(three_halves - 0.5 * dot3(z_parts, y_parts))
        root[...] = dot3(y_parts, f_parts)
        inverse[...] = dot3(f_parts, z_parts)
        return carry

    lax.fori_loop(0, STEPS - 2, newton_schulz, 0)
    y_parts, z_parts = two_parts(root[...]), two_parts(inverse[...])
    f_parts = two_parts(three_halves - 0.5 * dot3(z_parts, y_parts))
    z_parts = two_parts(dot3(f_parts, z_parts))
    scale = jnp.sqrt(ROWS / trace)

    columns = pl.ds(pl.multiple_of(128 * zb, 128), 128)
    second = Gather(pos, lambda index, h, k: iso_all.at[index, h, k], ring_sems[4:])

    def make_rows(b, c):
        for h in (0, 1):
            rows = pl.ds(pl.multiple_of(512 * b + 256 * c + HALF * h, HALF), HALF)
            a = (u_high[rows, :], u_low[rows, :])
            iso[core, b, c, h] = (dot3(a, z_parts) * scale).astype(BF16)

    def swap(n, s):
        block = (iso.at[s, half, 1 - s], iso.at[s, half, s], iso.at[s, 1 - half])[n]
        return remote(block, block, i_send.at[n], i_recv.at[n], sibling)

    make_rows(half, core)
    second.start(0, lambda k: iso.at[core, half, core, k, :, columns])
    make_rows(half, other)
    go(swap(0, core))
    for c in (0, 1):
        make_rows(1 - half, c)
    go(swap(1, core))
    go(swap(2, core))
    swap(0, other).wait_recv()
    second.start(1, lambda k: iso.at[other, half, core, k, :, columns])

    def swapped(n, term):
        return n == 0 or term == 0

    def to_pair(n, term):
        block = front.at[sectors[n], term, zb]
        return remote(block, block, f_send.at[n, term], f_recv.at[n, term], z_pair)

    def project(n, terms):
        rows = iso[sectors[n]].reshape(ROWS, COLS)
        for term in terms:
            front[sectors[n], term, zb] = dot_over_rows(left_v[sectors[n], term], rows).astype(BF16)
            if swapped(n, term):
                go(to_pair(n, term))
            else:
                front[sectors[n], term, 1 - zb] = dot_over_rows(left_pair[term - 1], rows).astype(BF16)

    project(0, (0, 1, 2))
    second.arrive(1)
    for n in (1, 2):
        swap(n, other).wait_recv()
    project(1, (0,))
    second.arrive(2)
    pair_blocks.wait_recv()
    project(1, (1, 2))
    own_rows = iso.at[:, x // 2, lax.rem(x, 2), z // 4, pl.ds(pl.multiple_of(32 * lax.rem(z, 4) + 16 * core, 16), 16)]
    out_iso = pltpu.make_async_copy(own_rows, iso_out, local_sem.at[6])
    own_block = pltpu.make_async_copy(
        iso.at[:, :, core, :, :, columns], iso_all.at[pl.ds(2 * y, 2)], local_sem.at[7]
    )
    out_iso.start()
    own_block.start()
    second.arrive(3)
    second.arrive(4)
    second.finish()
    own_block.wait()

    def to_sibling(n):
        s = sectors[n]
        return remote(e_out.at[s], e_in.at[s], e_send.at[n], e_recv.at[n], sibling)

    for n, s in enumerate(sectors):
        for term in range(3):
            if swapped(n, term):
                to_pair(n, term).wait_recv()
            source = shift[2 * y + s, 3 * group + term]
            rows = iso_all[source].reshape(512, 128)
            value = dot_over_rows(rows, front[s, term].reshape(512, COLS)) * (1 / 32)
            e_own[s, term] = jnp.where(core == 0, value[:64, :], value[64:, :])
            e_out[s, term] = jnp.where(core == 0, value[64:, :], value[:64, :]).astype(BF16)
        go(to_sibling(n))
    outs = [out_iso]
    for n in (0, 1):
        s = sectors[1 - n]
        remote(e_out.at[s], e_in.at[s], e_send.at[n], e_recv.at[n], sibling).wait_recv()
        env_v[s] = (e_own[s] + e_in[s].astype(F32)).astype(BF16)
        out_env = pltpu.make_async_copy(env_v.at[s], env_out.at[s], local_sem.at[8 + n])
        out_env.start()
        outs.append(out_env)

    for copy in waits + first.started + second.started:
        copy.wait_send()
    for copy in outs:
        copy.wait()


def body(wave_in, left_env, right_env, shift_map, live_rows):
    dma = pltpu.SemaphoreType.DMA
    anywhere = pl.BlockSpec(memory_space=pl.ANY)
    scratch = [
        pltpu.SMEM((16, 48), jnp.int32),
        pltpu.SMEM((16,), jnp.int32),
        pltpu.VMEM((2, 3, ROWS, COLS), BF16),
        pltpu.VMEM((ROWS, COLS), BF16),
        pltpu.VMEM((16, COLS, COLS), BF16),
        pltpu.VMEM((2, 3, COLS, COLS), BF16),
        pltpu.VMEM((2, 3, COLS, COLS), BF16),
        pltpu.VMEM((ROWS, COLS), BF16),
        pltpu.VMEM((ROWS, COLS), BF16),
        pltpu.VMEM((512, COLS), F32),
        pltpu.VMEM((3, 256, COLS), BF16),
        pltpu.VMEM((256, COLS), F32),
        pltpu.VMEM((3, 256, COLS), BF16),
        pltpu.VMEM((7, 32, COLS), BF16),
        pltpu.VMEM((32, COLS), F32),
        pltpu.VMEM((7, 32, COLS), BF16),
        pltpu.VMEM((2, ROWS, COLS), BF16),
        pltpu.VMEM((ROWS, COLS), BF16),
        pltpu.VMEM((ROWS, COLS), BF16),
        pltpu.VMEM((ROWS, COLS), BF16),
        pltpu.VMEM((COLS, COLS), F32),
        pltpu.VMEM((COLS, COLS), F32),
        pltpu.VMEM((2, 2, 2, 2, HALF, COLS), BF16),
        pltpu.VMEM((16, 2, 2, HALF, 128), BF16),
        pltpu.VMEM((2, 3, 2, COLS, COLS), BF16),
        pltpu.VMEM((2, 3, 64, COLS), BF16),
        pltpu.VMEM((2, 3, 64, COLS), BF16),
        pltpu.VMEM((2, 3, 64, COLS), F32),
        pltpu.VMEM((2, 3, 64, COLS), BF16),
        dma((10,)),
        *[dma((3,))] * 2,
        *[dma((2,))] * 2,
        *[dma((3, 4))] * 2,
        *[dma((7,))] * 2,
        *[dma((7,))] * 2,
        *[dma((3, 8))] * 2,
        *[dma((3,))] * 2,
        *[dma((2,))] * 2,
        *[dma((1,))] * 2,
        *[dma((2, 3))] * 2,
        *[dma((2, 4, 2, CHUNKS))] * 8,
    ]
    iso_rows, env_rows = pl.pallas_call(
        kernel,
        out_shape=(
            jax.ShapeDtypeStruct((2, 16, COLS), BF16),
            jax.ShapeDtypeStruct((2, 3, 64, COLS), BF16),
        ),
        in_specs=[anywhere] * 5,
        out_specs=(anywhere, anywhere),
        scratch_shapes=scratch,
        compiler_params=pltpu.CompilerParams(
            collective_id=0, has_side_effects=True, vmem_limit_bytes=60 * 2**20
        ),
        cost_estimate=pl.CostEstimate(flops=8 * 10**9, bytes_accessed=8 * 2**20, transcendentals=0),
        name="dmrg_window",
    )(shift_map.T, live_rows, wave_in, left_env, right_env.swapaxes(2, 3))
    return iso_rows, env_rows.swapaxes(2, 3)


def solution(mesh):
    split = Mesh(mesh.devices.reshape(NY, NX, NZ, 2), ("sector", *TERM))
    return jax.shard_map(
        body,
        mesh=split,
        in_specs=(
            P("sector", None, None),
            P("sector", TERM, None, None),
            P("sector", TERM, None, None),
            P(),
            P(),
        ),
        out_specs=(P("sector", TERM, None), P("sector", TERM, None, None)),
        check_vma=False,
    )
```

```python
import jax
import jax.numpy as jnp
from jax import lax
from jax.experimental import pallas as pl
from jax.experimental.pallas import tpu as pltpu
from jax.sharding import Mesh
from jax.sharding import PartitionSpec as P

STEPS = 8
NY, NX, NZ = 8, 4, 8
ROWS, COLS, HALF = 1024, 256, 128
CHUNKS = 2
CHUNK = HALF // CHUNKS
TERM = ("x", "z", "core")
STEP_SIZE = 0.15
EPSILON = 1e-06
MESH = pl.DeviceIdType.MESH
F32, BF16 = jnp.float32, jnp.bfloat16
FAR_FIRST = (4, 3, 5, 2, 6, 1, 7, 0)
X_FAR_FIRST = (2, 1, 3, 0)


def dot(a, b):
    return jnp.dot(a, b, preferred_element_type=F32)


def dot_over_rows(a, b):
    return lax.dot_general(a, b, (((0,), (0,)), ((), ())), preferred_element_type=F32)


def dot_over_columns(a, b):
    return lax.dot_general(a, b, (((1,), (1,)), ((), ())), preferred_element_type=F32)


def two_parts(a):
    high = a.astype(BF16)
    return high, (a - high.astype(F32)).astype(BF16)


def dot3(a, b):
    return dot(a[0], b[0]) + (dot(a[0], b[1]) + dot(a[1], b[0]))


def remote(src, dst, send, recv, to):
    return pltpu.make_async_remote_copy(
        src_ref=src, dst_ref=dst, send_sem=send, recv_sem=recv, device_id=to, device_id_type=MESH
    )


class Gather:
    def __init__(self, pos, chunk_at, sems):
        self.pos, self.chunk_at = pos, chunk_at
        self.y_send, self.y_recv, self.x_send, self.x_recv = sems
        self.half = lax.rem(pos["x"], 2)
        self.started = []

    def place(self, way, d, j, k, half):
        y, core = self.pos["sector"], self.pos["core"]
        step = d if way == 0 else NY - d
        sector = core if j == 0 else 1 - core
        index = 2 * lax.rem(y - step + 2 * NY, NY) + sector
        return self.chunk_at(index, half, k)

    def to(self, way, j):
        y, x = self.pos["sector"], self.pos["x"]
        at = dict(self.pos)
        if way is not None:
            at["sector"] = lax.rem(y + (1 if way == 0 else NY - 1), NY)
        if j is not None:
            at["x"] = lax.rem(x + (1 if j == 0 else NX - 1), NX)
        return at

    def neighbours(self):
        ways = ((0, None), (1, None), (None, 0), (None, 1), (0, 0), (0, 1), (1, 0), (1, 1))
        return [self.to(way, j) for way, j in ways]

    def go(self, copy):
        copy.start()
        self.started.append(copy)

    def along_y(self, source, way, d, j, k):
        at = (way, d, j, k)
        place = self.place(way, d, j, k, self.half)
        source = place if source is None else source
        self.go(remote(source, place, self.y_send.at[at], self.y_recv.at[at], self.to(way, None)))

    def along_x(self, way, d, j, k, ahead=False):
        at = (way, d if ahead else d - 1, j, k)
        block = self.place(way, d, j, k, self.half)
        self.go(remote(block, block, self.x_send.at[at], self.x_recv.at[at], self.to(way if ahead else None, j)))

    def wait_sends(self, keep=0):
        count = len(self.started) - keep
        for copy in self.started[:count]:
            copy.wait_send()
        del self.started[:count]

    def start(self, j, source):
        for k in range(CHUNKS):
            for way in (0, 1):
                self.along_y(source(k), way, 0, j, k)

    def arrive(self, d):
        for j in (0, 1):
            for k in range(CHUNKS):
                for way in (0, 1):
                    if d == 4 and j != way:
                        continue
                    at = (way, d - 1, j, k)
                    block = self.place(way, d, j, k, self.half)
                    remote(block, block, self.y_send.at[at], self.y_recv.at[at], self.to(way, None)).wait_recv()
                    if d < 3 or (d == 3 and j == way):
                        self.along_y(None, way, d, j, k)
                        if d == 3:
                            self.along_x(way, d, j, k, ahead=True)
                    if d < 4:
                        self.along_x(way, d, j, k)

    def finish(self):
        for d in (1, 2, 3, 4):
            for j in (0, 1):
                for k in range(CHUNKS):
                    for way in (0, 1):
                        if d == 4 and j != way:
                            continue
                        at = (way, d - 1, j, k)
                        block = self.place(way, d, j, k, 1 - self.half)
                        remote(block, block, self.x_send.at[at], self.x_recv.at[at], self.to(None, j)).wait_recv()


def kernel(
    shift_in,
    live_in,
    wave,
    left,
    right,
    iso_out,
    env_out,
    shift,
    live,
    left_v,
    wave_v,
    wave_all,
    right_all,
    applied,
    sib_out,
    sib_in,
    sigma,
    x_out,
    x_own,
    x_in,
    z_out,
    z_own,
    z_in,
    left_pair,
    total,
    u_high,
    u_low,
    root,
    inverse,
    iso,
    iso_all,
    front,
    e_out,
    e_in,
    e_own,
    env_v,
    local_sem,
    r_send,
    r_recv,
    sib_send,
    sib_recv,
    xs_send,
    xs_recv,
    zs_send,
    zs_recv,
    gz_send,
    gz_recv,
    gx_send,
    gx_recv,
    i_send,
    i_recv,
    e_send,
    e_recv,
    l_send,
    l_recv,
    f_send,
    f_recv,
    *ring_sems,
):
    y, x, z, core = (lax.axis_index(a) for a in ("sector", "x", "z", "core"))
    pos = {"sector": y, "x": x, "z": z, "core": core}
    zb = lax.rem(z, 2)
    part = 2 * zb + core
    group = 4 * x + z // 2
    half = lax.rem(x, 2)
    other = 1 - core
    sibling = {**pos, "core": other}
    z_pair = {**pos, "z": z + 1 - 2 * zb}
    x_to = [{**pos, "x": lax.rem(x + dx, NX)} for dx in range(NX)]
    z_to = [{**pos, "z": lax.rem(z + dz, NZ)} for dz in range(NZ)]
    sectors = (core, other)
    waits = []

    def go(copy):
        copy.start()
        waits.append(copy)
        return copy

    part_row = pl.multiple_of(part * COLS, COLS)
    own_left = pltpu.make_async_copy(left, left_v, local_sem.at[0])
    own_wave = pltpu.make_async_copy(wave.at[core], wave_v, local_sem.at[1])
    own_block = pltpu.make_async_copy(
        wave.at[:, pl.ds(part_row, COLS), :], wave_all.at[pl.ds(2 * y, 2)], local_sem.at[2]
    )

    own_shift = pltpu.make_async_copy(shift_in, shift, local_sem.at[4])
    own_live = pltpu.make_async_copy(live_in, live, local_sem.at[5])

    def wave_chunk(index, h, k):
        return wave_all.at[index, pl.ds(pl.multiple_of(h * HALF + k * CHUNK, CHUNK), CHUNK), :]

    first = Gather(pos, wave_chunk, ring_sems[:4])
    barrier = pltpu.get_barrier_semaphore()
    partners = first.neighbours() + [sibling, x_to[2]] + z_to[1:]
    for to in partners:
        pl.semaphore_signal(barrier, inc=1, device_id=to, device_id_type=MESH)
    pl.semaphore_wait(barrier, len(partners))

    send_row = part * COLS + half * HALF
    for j in (0, 1):
        first.start(j, lambda k: wave.at[sectors[j], pl.ds(pl.multiple_of(send_row + CHUNK * k, CHUNK), CHUNK), :])

    def right_rows(p):
        return right_all.at[:, :, pl.ds(pl.multiple_of(64 * p, 64), 64), :]

    mine = right_rows(part)
    own_right = pltpu.make_async_copy(right, mine, local_sem.at[3])
    go(remote(right, mine, r_send.at[1], r_recv.at[1], z_pair))
    go(remote(right, mine, r_send.at[0], r_recv.at[0], sibling))
    for copy in (own_shift, own_live, own_block, own_right, own_left, own_wave):
        copy.start()
    first.arrive(1)
    pair_blocks = remote(left.at[other, pl.ds(1, 2)], left_pair, l_send.at[0], l_recv.at[0], z_pair)
    go(pair_blocks)
    first.arrive(2)
    far = right_rows(2 * (1 - zb) + core)
    remote(far, far, r_send.at[1], r_recv.at[1], z_pair).wait_recv()
    go(remote(far, far, r_send.at[2], r_recv.at[2], sibling))
    first.arrive(3)
    near = right_rows(2 * zb + other)
    remote(near, near, r_send.at[0], r_recv.at[0], sibling).wait_recv()
    last = right_rows(2 * (1 - zb) + other)
    remote(last, last, r_send.at[2], r_recv.at[2], sibling).wait_recv()
    for copy in (own_shift, own_live, own_block, own_right, own_left, own_wave):
        copy.wait()
    first.arrive(4)
    first.finish()

    def row_order(dx):
        base = 256 * lax.rem(x + dx, NX)
        return [pl.ds(pl.multiple_of(base + 32 * lax.rem(z + dz, NZ), 32), 32) for dz in FAR_FIRST]

    def partial_sum(s, dx):
        pieces = row_order(dx)
        acc = jnp.zeros((256, COLS), F32)
        for term in range(3):
            rows = jnp.concatenate([left_v[s, term, p, :] for p in pieces], axis=0)
            acc = acc + dot(rows, applied[s, term])
        return acc

    def apply(s):
        for term in range(3):
            source = shift[2 * y + s, 3 * group + term]
            applied[s, term] = dot_over_columns(wave_all[source], right_all[s, term]).astype(BF16)

    def from_sibling_sum(q):
        h = pl.ds(512 * q, 512)
        return remote(sib_out.at[h], sib_in.at[h], sib_send.at[q], sib_recv.at[q], sibling)

    apply(other)
    for i, dx in enumerate(X_FAR_FIRST):
        sib_out[256 * i : 256 * (i + 1), :] = partial_sum(other, dx).astype(BF16)
        if i % 2 == 1:
            go(from_sibling_sum(i // 2))
    apply(core)
    for i in (0, 1):
        sigma[256 * i : 256 * (i + 1), :] = partial_sum(core, X_FAR_FIRST[i])

    def to_x(dx, g):
        h = pl.ds(64 * g, 64)
        return remote(
            x_out.at[dx - 1, h], x_in.at[dx - 1, h], xs_send.at[dx - 1, g], xs_recv.at[dx - 1, g], x_to[dx]
        )

    for i, dx in enumerate(X_FAR_FIRST):
        if i % 2 == 0:
            from_sibling_sum(i // 2).wait_recv()
        if i < 2:
            acc = sigma[256 * i : 256 * (i + 1), :]
        else:
            acc = partial_sum(core, dx)
        acc = acc + sib_in[256 * i : 256 * (i + 1), :].astype(F32)
        if dx == 0:
            x_own[...] = acc
            continue
        x_out[dx - 1] = acc.astype(BF16)
        for g in range(4):
            go(to_x(dx, g))
    for g in range(4):
        slots = (2 * g, 2 * g + 1)
        rows = slice(64 * g, 64 * (g + 1))
        acc = x_own[rows, :]
        for dx in (1, 2, 3):
            to_x(dx, g).wait_recv()
            acc = acc + x_in[dx - 1, rows, :].astype(F32)
        for i in slots:
            piece = acc[32 * (i - slots[0]) : 32 * (i - slots[0] + 1), :]
            if FAR_FIRST[i]:
                z_out[i] = piece.astype(BF16)
                go(remote(z_out.at[i], z_in.at[i], zs_send.at[i], zs_recv.at[i], z_to[FAR_FIRST[i]]))
            else:
                z_own[...] = piece
    acc = z_own[...]
    for i in range(7):
        remote(z_out.at[i], z_in.at[i], zs_send.at[i], zs_recv.at[i], z_to[FAR_FIRST[i]]).wait_recv()
        acc = acc + z_in[i].astype(F32)

    def piece_at(dx, dz):
        at = 256 * lax.rem(x + NX - dx, NX) + 32 * lax.rem(z + NZ - dz, NZ)
        return total.at[pl.ds(pl.multiple_of(at, 32), 32)]

    own_piece = piece_at(0, 0)
    own_piece[...] = acc.astype(BF16)
    for i in range(7):
        go(remote(own_piece, own_piece, gz_send.at[i], gz_recv.at[i], z_to[FAR_FIRST[i]]))
    for i in range(7, -1, -1):
        piece = piece_at(0, FAR_FIRST[i])
        if i < 7:
            remote(piece, piece, gz_send.at[i], gz_recv.at[i], z_to[FAR_FIRST[i]]).wait_recv()
        for dx in (2, 1, 3):
            go(remote(piece, piece, gx_send.at[dx - 1, i], gx_recv.at[dx - 1, i], x_to[dx]))

    limit = live[2 * y + core]
    gram = jnp.zeros((COLS, COLS), F32)
    cross = jnp.zeros((COLS, COLS), F32)
    for dx in (0, 1, 3, 2):
        if dx:
            for i in range(7, -1, -1):
                piece = piece_at(dx, FAR_FIRST[i])
                remote(piece, piece, gx_send.at[dx - 1, i], gx_recv.at[dx - 1, i], x_to[dx]).wait_recv()
        base = pl.multiple_of(256 * lax.rem(x + NX - dx, NX), 256)
        rows = pl.ds(base, 256)
        row_ids = base + lax.broadcasted_iota(jnp.int32, (256, COLS), 0)
        value = wave_v[rows, :].astype(F32) - STEP_SIZE * total[rows, :].astype(F32)
        high, low = two_parts(jnp.where(row_ids < limit, value, 0.0))
        u_high[rows, :] = high
        u_low[rows, :] = low
        gram = gram + dot_over_rows(high, high)
        cross = cross + dot_over_rows(high, low)
    gram = gram + (cross + cross.T)
    diagonal = lax.broadcasted_iota(jnp.int32, (COLS, COLS), 0) == lax.broadcasted_iota(jnp.int32, (COLS, COLS), 1)
    trace = jnp.sum(jnp.where(diagonal, gram, 0.0), keepdims=True) + EPSILON
    three_halves = jnp.where(diagonal, 1.5, 0.0)
    y0 = gram / trace
    factor = three_halves - 0.5 * y0
    root[...] = dot3(two_parts(y0), two_parts(factor))
    inverse[...] = factor

    def newton_schulz(_, carry):
        y_parts, z_parts = two_parts(root[...]), two_parts(inverse[...])
        f_parts = two_parts(three_halves - 0.5 * dot3(z_parts, y_parts))
        root[...] = dot3(y_parts, f_parts)
        inverse[...] = dot3(f_parts, z_parts)
        return carry

    lax.fori_loop(0, STEPS - 2, newton_schulz, 0)
    y_parts, z_parts = two_parts(root[...]), two_parts(inverse[...])
    f_parts = two_parts(three_halves - 0.5 * dot3(z_parts, y_parts))
    z_parts = two_parts(dot3(f_parts, z_parts))
    scale = jnp.sqrt(ROWS / trace)

    columns = pl.ds(pl.multiple_of(128 * zb, 128), 128)
    second = Gather(pos, lambda index, h, k: iso_all.at[index, h, k], ring_sems[4:])

    def make_rows(b, c):
        for h in (0, 1):
            rows = pl.ds(pl.multiple_of(512 * b + 256 * c + HALF * h, HALF), HALF)
            a = (u_high[rows, :], u_low[rows, :])
            iso[core, b, c, h] = (dot3(a, z_parts) * scale).astype(BF16)

    def swap(n, s):
        block = (iso.at[s, half, 1 - s], iso.at[s, half, s], iso.at[s, 1 - half])[n]
        return remote(block, block, i_send.at[n], i_recv.at[n], sibling)

    make_rows(half, core)
    second.start(0, lambda k: iso.at[core, half, core, k, :, columns])
    make_rows(half, other)
    go(swap(0, core))
    for c in (0, 1):
        make_rows(1 - half, c)
    go(swap(1, core))
    go(swap(2, core))
    swap(0, other).wait_recv()
    second.start(1, lambda k: iso.at[other, half, core, k, :, columns])

    def swapped(n, term):
        return n == 0 or term == 0

    def to_pair(n, term):
        block = front.at[sectors[n], term, zb]
        return remote(block, block, f_send.at[n, term], f_recv.at[n, term], z_pair)

    def project(n, terms):
        rows = iso[sectors[n]].reshape(ROWS, COLS)
        for term in terms:
            front[sectors[n], term, zb] = dot_over_rows(left_v[sectors[n], term], rows).astype(BF16)
            if swapped(n, term):
                go(to_pair(n, term))
            else:
                front[sectors[n], term, 1 - zb] = dot_over_rows(left_pair[term - 1], rows).astype(BF16)

    project(0, (0, 1, 2))
    second.arrive(1)
    for n in (1, 2):
        swap(n, other).wait_recv()
    project(1, (0,))
    first.wait_sends()
    second.arrive(2)
    pair_blocks.wait_recv()
    project(1, (1, 2))
    own_rows = iso.at[:, x // 2, lax.rem(x, 2), z // 4, pl.ds(pl.multiple_of(32 * lax.rem(z, 4) + 16 * core, 16), 16)]
    out_iso = pltpu.make_async_copy(own_rows, iso_out, local_sem.at[6])
    own_block = pltpu.make_async_copy(
        iso.at[:, :, core, :, :, columns], iso_all.at[pl.ds(2 * y, 2)], local_sem.at[7]
    )
    out_iso.start()
    own_block.start()
    for copy in waits:
        copy.wait_send()
    waits.clear()
    second.arrive(3)
    second.wait_sends(keep=36)
    second.arrive(4)
    second.finish()
    own_block.wait()

    def to_sibling(n, s, term):
        at = (s, term)
        return remote(e_out.at[at], e_in.at[at], e_send.at[n, term], e_recv.at[n, term], sibling)

    for n, s in enumerate(sectors):
        for term in range(3):
            if swapped(n, term):
                to_pair(n, term).wait_recv()
            source = shift[2 * y + s, 3 * group + term]
            rows = iso_all[source].reshape(512, 128)
            value = dot_over_rows(rows, front[s, term].reshape(512, COLS)) * (1 / 32)
            e_own[s, term] = jnp.where(core == 0, value[:64, :], value[64:, :])
            e_out[s, term] = jnp.where(core == 0, value[64:, :], value[:64, :]).astype(BF16)
            go(to_sibling(n, s, term))
    outs = [out_iso]
    for n in (0, 1):
        s = sectors[1 - n]
        for term in range(3):
            to_sibling(n, s, term).wait_recv()
        env_v[s] = (e_own[s] + e_in[s].astype(F32)).astype(BF16)
        out_env = pltpu.make_async_copy(env_v.at[s], env_out.at[s], local_sem.at[8 + n])
        out_env.start()
        outs.append(out_env)

    for copy in waits + second.started:
        copy.wait_send()
    for copy in outs:
        copy.wait()


def body(wave_in, left_env, right_env, shift_map, live_rows):
    dma = pltpu.SemaphoreType.DMA
    anywhere = pl.BlockSpec(memory_space=pl.ANY)
    scratch = [
        pltpu.SMEM((16, 48), jnp.int32),
        pltpu.SMEM((16,), jnp.int32),
        pltpu.VMEM((2, 3, ROWS, COLS), BF16),
        pltpu.VMEM((ROWS, COLS), BF16),
        pltpu.VMEM((16, COLS, COLS), BF16),
        pltpu.VMEM((2, 3, COLS, COLS), BF16),
        pltpu.VMEM((2, 3, COLS, COLS), BF16),
        pltpu.VMEM((ROWS, COLS), BF16),
        pltpu.VMEM((ROWS, COLS), BF16),
        pltpu.VMEM((512, COLS), F32),
        pltpu.VMEM((3, 256, COLS), BF16),
        pltpu.VMEM((256, COLS), F32),
        pltpu.VMEM((3, 256, COLS), BF16),
        pltpu.VMEM((7, 32, COLS), BF16),
        pltpu.VMEM((32, COLS), F32),
        pltpu.VMEM((7, 32, COLS), BF16),
        pltpu.VMEM((2, ROWS, COLS), BF16),
        pltpu.VMEM((ROWS, COLS), BF16),
        pltpu.VMEM((ROWS, COLS), BF16),
        pltpu.VMEM((ROWS, COLS), BF16),
        pltpu.VMEM((COLS, COLS), F32),
        pltpu.VMEM((COLS, COLS), F32),
        pltpu.VMEM((2, 2, 2, 2, HALF, COLS), BF16),
        pltpu.VMEM((16, 2, 2, HALF, 128), BF16),
        pltpu.VMEM((2, 3, 2, COLS, COLS), BF16),
        pltpu.VMEM((2, 3, 64, COLS), BF16),
        pltpu.VMEM((2, 3, 64, COLS), BF16),
        pltpu.VMEM((2, 3, 64, COLS), F32),
        pltpu.VMEM((2, 3, 64, COLS), BF16),
        dma((10,)),
        *[dma((3,))] * 2,
        *[dma((2,))] * 2,
        *[dma((3, 4))] * 2,
        *[dma((7,))] * 2,
        *[dma((7,))] * 2,
        *[dma((3, 8))] * 2,
        *[dma((3,))] * 2,
        *[dma((2, 3))] * 2,
        *[dma((1,))] * 2,
        *[dma((2, 3))] * 2,
        *[dma((2, 4, 2, CHUNKS))] * 8,
    ]
    iso_rows, env_rows = pl.pallas_call(
        kernel,
        out_shape=(
            jax.ShapeDtypeStruct((2, 16, COLS), BF16),
            jax.ShapeDtypeStruct((2, 3, 64, COLS), BF16),
        ),
        in_specs=[anywhere] * 5,
        out_specs=(anywhere, anywhere),
        scratch_shapes=scratch,
        compiler_params=pltpu.CompilerParams(
            collective_id=0, has_side_effects=True, vmem_limit_bytes=60 * 2**20
        ),
        cost_estimate=pl.CostEstimate(flops=8 * 10**9, bytes_accessed=8 * 2**20, transcendentals=0),
        name="dmrg_window",
    )(shift_map.T, live_rows, wave_in, left_env, right_env.swapaxes(2, 3))
    return iso_rows, env_rows.swapaxes(2, 3)


def solution(mesh):
    split = Mesh(mesh.devices.reshape(NY, NX, NZ, 2), ("sector", *TERM))
    return jax.shard_map(
        body,
        mesh=split,
        in_specs=(
            P("sector", None, None),
            P("sector", TERM, None, None),
            P("sector", TERM, None, None),
            P(),
            P(),
        ),
        out_specs=(P("sector", TERM, None), P("sector", TERM, None, None)),
        check_vma=False,
    )
```

```python
import jax
import jax.numpy as jnp
from jax import lax
from jax.experimental import pallas as pl
from jax.experimental.pallas import tpu as pltpu
from jax.sharding import Mesh
from jax.sharding import PartitionSpec as P

STEPS = 8
NY, NX, NZ = 8, 4, 8
ROWS, COLS, HALF = 1024, 256, 128
CHUNKS = 2
CHUNK = HALF // CHUNKS
TERM = ("x", "z", "core")
STEP_SIZE = 0.15
EPSILON = 1e-06
MESH = pl.DeviceIdType.MESH
F32, BF16 = jnp.float32, jnp.bfloat16
FAR_FIRST = (4, 3, 5, 2, 6, 1, 7, 0)
X_FAR_FIRST = (2, 1, 3, 0)


def dot(a, b):
    return jnp.dot(a, b, preferred_element_type=F32)


def dot_over_rows(a, b):
    return lax.dot_general(a, b, (((0,), (0,)), ((), ())), preferred_element_type=F32)


def dot_over_columns(a, b):
    return lax.dot_general(a, b, (((1,), (1,)), ((), ())), preferred_element_type=F32)


def two_parts(a):
    high = a.astype(BF16)
    return high, (a - high.astype(F32)).astype(BF16)


def dot3(a, b):
    return dot(a[0], b[0]) + (dot(a[0], b[1]) + dot(a[1], b[0]))


def remote(src, dst, send, recv, to):
    return pltpu.make_async_remote_copy(
        src_ref=src, dst_ref=dst, send_sem=send, recv_sem=recv, device_id=to, device_id_type=MESH
    )


class Gather:
    def __init__(self, pos, chunk_at, sems):
        self.pos, self.chunk_at = pos, chunk_at
        self.y_send, self.y_recv, self.x_send, self.x_recv = sems
        self.half = lax.rem(pos["x"], 2)
        self.started = []

    def place(self, way, d, j, k, half):
        y, core = self.pos["sector"], self.pos["core"]
        step = d if way == 0 else NY - d
        sector = core if j == 0 else 1 - core
        index = 2 * lax.rem(y - step + 2 * NY, NY) + sector
        return self.chunk_at(index, half, k)

    def to(self, way, j):
        y, x = self.pos["sector"], self.pos["x"]
        at = dict(self.pos)
        if way is not None:
            at["sector"] = lax.rem(y + (1 if way == 0 else NY - 1), NY)
        if j is not None:
            at["x"] = lax.rem(x + (1 if j == 0 else NX - 1), NX)
        return at

    def neighbours(self):
        ways, sides = (0, 1, None), (0, 1, None)
        return [self.to(w, j) for w in ways for j in sides if w is not None or j is not None]

    def go(self, copy):
        copy.start()
        self.started.append(copy)

    def along_y(self, source, way, d, j, k):
        at = (way, d, j, k)
        place = self.place(way, d, j, k, self.half)
        source = place if source is None else source
        self.go(remote(source, place, self.y_send.at[at], self.y_recv.at[at], self.to(way, None)))

    def along_x(self, way, d, j, k, ahead=False):
        at = (way, d if ahead else d - 1, j, k)
        block = self.place(way, d, j, k, self.half)
        self.go(remote(block, block, self.x_send.at[at], self.x_recv.at[at], self.to(way if ahead else None, j)))

    def start(self, j, source):
        for k in range(CHUNKS):
            for way in (0, 1):
                self.along_y(source(k), way, 0, j, k)

    def arrive(self, d):
        for j in (0, 1):
            for k in range(CHUNKS):
                for way in (0, 1):
                    if d == 4 and j != way:
                        continue
                    at = (way, d - 1, j, k)
                    block = self.place(way, d, j, k, self.half)
                    remote(block, block, self.y_send.at[at], self.y_recv.at[at], self.to(way, None)).wait_recv()
                    if d < 3 or (d == 3 and j == way):
                        self.along_y(None, way, d, j, k)
                        if d == 3:
                            self.along_x(way, d, j, k, ahead=True)
                    if d < 4:
                        self.along_x(way, d, j, k)

    def finish(self):
        for d in (1, 2, 3, 4):
            for j in (0, 1):
                for k in range(CHUNKS):
                    for way in (0, 1):
                        if d == 4 and j != way:
                            continue
                        at = (way, d - 1, j, k)
                        block = self.place(way, d, j, k, 1 - self.half)
                        remote(block, block, self.x_send.at[at], self.x_recv.at[at], self.to(None, j)).wait_recv()


def kernel(
    shift_in,
    live_in,
    wave,
    left,
    right,
    iso_out,
    env_out,
    shift,
    live,
    left_v,
    wave_v,
    wave_all,
    right_all,
    applied,
    sib_out,
    sib_in,
    sigma,
    x_out,
    x_own,
    x_in,
    z_out,
    z_own,
    z_in,
    left_pair,
    total,
    u_high,
    u_low,
    root,
    inverse,
    iso,
    iso_all,
    front,
    e_out,
    e_in,
    e_own,
    env_v,
    local_sem,
    r_send,
    r_recv,
    sib_send,
    sib_recv,
    xs_send,
    xs_recv,
    zs_send,
    zs_recv,
    gz_send,
    gz_recv,
    gx_send,
    gx_recv,
    i_send,
    i_recv,
    e_send,
    e_recv,
    l_send,
    l_recv,
    f_send,
    f_recv,
    *ring_sems,
):
    y, x, z, core = (lax.axis_index(a) for a in ("sector", "x", "z", "core"))
    pos = {"sector": y, "x": x, "z": z, "core": core}
    zb = lax.rem(z, 2)
    part = 2 * zb + core
    group = 4 * x + z // 2
    half = lax.rem(x, 2)
    other = 1 - core
    sibling = {**pos, "core": other}
    z_pair = {**pos, "z": z + 1 - 2 * zb}
    x_to = [{**pos, "x": lax.rem(x + dx, NX)} for dx in range(NX)]
    z_to = [{**pos, "z": lax.rem(z + dz, NZ)} for dz in range(NZ)]
    sectors = (core, other)
    waits = []

    def go(copy):
        copy.start()
        waits.append(copy)
        return copy

    part_row = pl.multiple_of(part * COLS, COLS)
    own_left = pltpu.make_async_copy(left, left_v, local_sem.at[0])
    own_wave = pltpu.make_async_copy(wave.at[core], wave_v, local_sem.at[1])
    own_block = pltpu.make_async_copy(
        wave.at[:, pl.ds(part_row, COLS), :], wave_all.at[pl.ds(2 * y, 2)], local_sem.at[2]
    )

    own_shift = pltpu.make_async_copy(shift_in, shift, local_sem.at[4])
    own_live = pltpu.make_async_copy(live_in, live, local_sem.at[5])

    def wave_chunk(index, h, k):
        return wave_all.at[index, pl.ds(pl.multiple_of(h * HALF + k * CHUNK, CHUNK), CHUNK), :]

    first = Gather(pos, wave_chunk, ring_sems[:4])
    barrier = pltpu.get_barrier_semaphore()
    partners = first.neighbours() + [sibling, x_to[2]] + z_to[1:]
    for to in partners:
        pl.semaphore_signal(barrier, inc=1, device_id=to, device_id_type=MESH)
    pl.semaphore_wait(barrier, len(partners))

    send_row = part * COLS + half * HALF
    for j in (0, 1):
        first.start(j, lambda k: wave.at[sectors[j], pl.ds(pl.multiple_of(send_row + CHUNK * k, CHUNK), CHUNK), :])

    def right_rows(p):
        return right_all.at[:, :, pl.ds(pl.multiple_of(64 * p, 64), 64), :]

    mine = right_rows(part)
    own_right = pltpu.make_async_copy(right, mine, local_sem.at[3])
    go(remote(right, mine, r_send.at[1], r_recv.at[1], z_pair))
    go(remote(right, mine, r_send.at[0], r_recv.at[0], sibling))
    for copy in (own_shift, own_live, own_block, own_right, own_left, own_wave):
        copy.start()
    pair_blocks = remote(left.at[other, pl.ds(1, 2)], left_pair, l_send.at[0], l_recv.at[0], z_pair)
    go(pair_blocks)
    first.arrive(1)
    first.arrive(2)
    far = right_rows(2 * (1 - zb) + core)
    remote(far, far, r_send.at[1], r_recv.at[1], z_pair).wait_recv()
    go(remote(far, far, r_send.at[2], r_recv.at[2], sibling))
    first.arrive(3)
    near = right_rows(2 * zb + other)
    remote(near, near, r_send.at[0], r_recv.at[0], sibling).wait_recv()
    last = right_rows(2 * (1 - zb) + other)
    remote(last, last, r_send.at[2], r_recv.at[2], sibling).wait_recv()
    for copy in (own_shift, own_live, own_block, own_right, own_left, own_wave):
        copy.wait()
    first.arrive(4)
    first.finish()

    def row_order(dx):
        base = 256 * lax.rem(x + dx, NX)
        return [pl.ds(pl.multiple_of(base + 32 * lax.rem(z + dz, NZ), 32), 32) for dz in FAR_FIRST]

    def partial_sum(s, dx):
        pieces = row_order(dx)
        acc = jnp.zeros((256, COLS), F32)
        for term in range(3):
            rows = jnp.concatenate([left_v[s, term, p, :] for p in pieces], axis=0)
            acc = acc + dot(rows, applied[s, term])
        return acc

    def apply(s):
        for term in range(3):
            source = shift[2 * y + s, 3 * group + term]
            applied[s, term] = dot_over_columns(wave_all[source], right_all[s, term]).astype(BF16)

    def from_sibling_sum(q):
        h = pl.ds(512 * q, 512)
        return remote(sib_out.at[h], sib_in.at[h], sib_send.at[q], sib_recv.at[q], sibling)

    apply(other)
    for i, dx in enumerate(X_FAR_FIRST):
        sib_out[256 * i : 256 * (i + 1), :] = partial_sum(other, dx).astype(BF16)
        if i % 2 == 1:
            go(from_sibling_sum(i // 2))
    apply(core)
    for i in (0, 1):
        sigma[256 * i : 256 * (i + 1), :] = partial_sum(core, X_FAR_FIRST[i])

    def to_x(dx, g):
        h = pl.ds(64 * g, 64)
        return remote(
            x_out.at[dx - 1, h], x_in.at[dx - 1, h], xs_send.at[dx - 1, g], xs_recv.at[dx - 1, g], x_to[dx]
        )

    for i, dx in enumerate(X_FAR_FIRST):
        if i % 2 == 0:
            from_sibling_sum(i // 2).wait_recv()
        if i < 2:
            acc = sigma[256 * i : 256 * (i + 1), :]
        else:
            acc = partial_sum(core, dx)
        acc = acc + sib_in[256 * i : 256 * (i + 1), :].astype(F32)
        if dx == 0:
            x_own[...] = acc
            continue
        x_out[dx - 1] = acc.astype(BF16)
        for g in range(4):
            go(to_x(dx, g))
    for g in range(4):
        slots = (2 * g, 2 * g + 1)
        rows = slice(64 * g, 64 * (g + 1))
        acc = x_own[rows, :]
        for dx in (1, 2, 3):
            to_x(dx, g).wait_recv()
            acc = acc + x_in[dx - 1, rows, :].astype(F32)
        for i in slots:
            piece = acc[32 * (i - slots[0]) : 32 * (i - slots[0] + 1), :]
            if FAR_FIRST[i]:
                z_out[i] = piece.astype(BF16)
                go(remote(z_out.at[i], z_in.at[i], zs_send.at[i], zs_recv.at[i], z_to[FAR_FIRST[i]]))
            else:
                z_own[...] = piece
    acc = z_own[...]
    for i in range(7):
        remote(z_out.at[i], z_in.at[i], zs_send.at[i], zs_recv.at[i], z_to[FAR_FIRST[i]]).wait_recv()
        acc = acc + z_in[i].astype(F32)

    def piece_at(dx, dz):
        at = 256 * lax.rem(x + NX - dx, NX) + 32 * lax.rem(z + NZ - dz, NZ)
        return total.at[pl.ds(pl.multiple_of(at, 32), 32)]

    own_piece = piece_at(0, 0)
    own_piece[...] = acc.astype(BF16)
    for i in range(7):
        go(remote(own_piece, own_piece, gz_send.at[i], gz_recv.at[i], z_to[FAR_FIRST[i]]))
    for i in range(7, -1, -1):
        piece = piece_at(0, FAR_FIRST[i])
        if i < 7:
            remote(piece, piece, gz_send.at[i], gz_recv.at[i], z_to[FAR_FIRST[i]]).wait_recv()
        for dx in (2, 1, 3):
            go(remote(piece, piece, gx_send.at[dx - 1, i], gx_recv.at[dx - 1, i], x_to[dx]))

    limit = live[2 * y + core]
    gram = jnp.zeros((COLS, COLS), F32)
    cross = jnp.zeros((COLS, COLS), F32)
    for dx in (0, 1, 3, 2):
        if dx:
            for i in range(7, -1, -1):
                piece = piece_at(dx, FAR_FIRST[i])
                remote(piece, piece, gx_send.at[dx - 1, i], gx_recv.at[dx - 1, i], x_to[dx]).wait_recv()
        base = pl.multiple_of(256 * lax.rem(x + NX - dx, NX), 256)
        rows = pl.ds(base, 256)
        row_ids = base + lax.broadcasted_iota(jnp.int32, (256, COLS), 0)
        value = wave_v[rows, :].astype(F32) - STEP_SIZE * total[rows, :].astype(F32)
        high, low = two_parts(jnp.where(row_ids < limit, value, 0.0))
        u_high[rows, :] = high
        u_low[rows, :] = low
        gram = gram + dot_over_rows(high, high)
        cross = cross + dot_over_rows(high, low)
    gram = gram + (cross + cross.T)
    diagonal = lax.broadcasted_iota(jnp.int32, (COLS, COLS), 0) == lax.broadcasted_iota(jnp.int32, (COLS, COLS), 1)
    trace = jnp.sum(jnp.where(diagonal, gram, 0.0), keepdims=True) + EPSILON
    three_halves = jnp.where(diagonal, 1.5, 0.0)
    y0 = gram / trace
    factor = three_halves - 0.5 * y0
    root[...] = dot3(two_parts(y0), two_parts(factor))
    inverse[...] = factor

    def newton_schulz(_, carry):
        y_parts, z_parts = two_parts(root[...]), two_parts(inverse[...])
        f_parts = two_parts(three_halves - 0.5 * dot3(z_parts, y_parts))
        root[...] = dot3(y_parts, f_parts)
        inverse[...] = dot3(f_parts, z_parts)
        return carry

    lax.fori_loop(0, STEPS - 2, newton_schulz, 0)
    y_parts, z_parts = two_parts(root[...]), two_parts(inverse[...])
    f_parts = two_parts(three_halves - 0.5 * dot3(z_parts, y_parts))
    z_parts = two_parts(dot3(f_parts, z_parts))
    scale = jnp.sqrt(ROWS / trace)

    columns = pl.ds(pl.multiple_of(128 * zb, 128), 128)
    second = Gather(pos, lambda index, h, k: iso_all.at[index, h, k], ring_sems[4:])

    def make_rows(b, c):
        for h in (0, 1):
            rows = pl.ds(pl.multiple_of(512 * b + 256 * c + HALF * h, HALF), HALF)
            a = (u_high[rows, :], u_low[rows, :])
            iso[core, b, c, h] = (dot3(a, z_parts) * scale).astype(BF16)

    def swap(n, s):
        block = (iso.at[s, half, 1 - s], iso.at[s, half, s], iso.at[s, 1 - half])[n]
        return remote(block, block, i_send.at[n], i_recv.at[n], sibling)

    make_rows(half, core)
    second.start(0, lambda k: iso.at[core, half, core, k, :, columns])
    make_rows(half, other)
    go(swap(0, core))
    for c in (0, 1):
        make_rows(1 - half, c)
    go(swap(1, core))
    go(swap(2, core))
    swap(0, other).wait_recv()
    second.start(1, lambda k: iso.at[other, half, core, k, :, columns])

    def swapped(n, term):
        return n == 0 or term == 0

    def to_pair(n, term):
        block = front.at[sectors[n], term, zb]
        return remote(block, block, f_send.at[n, term], f_recv.at[n, term], z_pair)

    def project(n, terms):
        rows = iso[sectors[n]].reshape(ROWS, COLS)
        for term in terms:
            front[sectors[n], term, zb] = dot_over_rows(left_v[sectors[n], term], rows).astype(BF16)
            if swapped(n, term):
                go(to_pair(n, term))
            else:
                front[sectors[n], term, 1 - zb] = dot_over_rows(left_pair[term - 1], rows).astype(BF16)

    project(0, (0, 1, 2))
    second.arrive(1)
    for n in (1, 2):
        swap(n, other).wait_recv()
    project(1, (0,))
    second.arrive(2)
    pair_blocks.wait_recv()
    project(1, (1, 2))
    own_rows = iso.at[:, x // 2, lax.rem(x, 2), z // 4, pl.ds(pl.multiple_of(32 * lax.rem(z, 4) + 16 * core, 16), 16)]
    out_iso = pltpu.make_async_copy(own_rows, iso_out, local_sem.at[6])
    own_block = pltpu.make_async_copy(
        iso.at[:, :, core, :, :, columns], iso_all.at[pl.ds(2 * y, 2)], local_sem.at[7]
    )
    out_iso.start()
    own_block.start()
    second.arrive(3)
    second.arrive(4)
    second.finish()
    own_block.wait()

    def to_sibling(n):
        s = sectors[n]
        return remote(e_out.at[s], e_in.at[s], e_send.at[n], e_recv.at[n], sibling)

    for n, s in enumerate(sectors):
        for term in range(3):
            if swapped(n, term):
                to_pair(n, term).wait_recv()
            source = shift[2 * y + s, 3 * group + term]
            rows = iso_all[source].reshape(512, 128)
            value = dot_over_rows(rows, front[s, term].reshape(512, COLS)) * (1 / 32)
            e_own[s, term] = jnp.where(core == 0, value[:64, :], value[64:, :])
            e_out[s, term] = jnp.where(core == 0, value[64:, :], value[:64, :]).astype(BF16)
        go(to_sibling(n))
    outs = [out_iso]
    for n in (0, 1):
        s = sectors[1 - n]
        remote(e_out.at[s], e_in.at[s], e_send.at[n], e_recv.at[n], sibling).wait_recv()
        env_v[s] = (e_own[s] + e_in[s].astype(F32)).astype(BF16)
        out_env = pltpu.make_async_copy(env_v.at[s], env_out.at[s], local_sem.at[8 + n])
        out_env.start()
        outs.append(out_env)

    for copy in waits + first.started + second.started:
        copy.wait_send()
    for copy in outs:
        copy.wait()


def body(wave_in, left_env, right_env, shift_map, live_rows):
    dma = pltpu.SemaphoreType.DMA
    anywhere = pl.BlockSpec(memory_space=pl.ANY)
    scratch = [
        pltpu.SMEM((16, 48), jnp.int32),
        pltpu.SMEM((16,), jnp.int32),
        pltpu.VMEM((2, 3, ROWS, COLS), BF16),
        pltpu.VMEM((ROWS, COLS), BF16),
        pltpu.VMEM((16, COLS, COLS), BF16),
        pltpu.VMEM((2, 3, COLS, COLS), BF16),
        pltpu.VMEM((2, 3, COLS, COLS), BF16),
        pltpu.VMEM((ROWS, COLS), BF16),
        pltpu.VMEM((ROWS, COLS), BF16),
        pltpu.VMEM((512, COLS), F32),
        pltpu.VMEM((3, 256, COLS), BF16),
        pltpu.VMEM((256, COLS), F32),
        pltpu.VMEM((3, 256, COLS), BF16),
        pltpu.VMEM((7, 32, COLS), BF16),
        pltpu.VMEM((32, COLS), F32),
        pltpu.VMEM((7, 32, COLS), BF16),
        pltpu.VMEM((2, ROWS, COLS), BF16),
        pltpu.VMEM((ROWS, COLS), BF16),
        pltpu.VMEM((ROWS, COLS), BF16),
        pltpu.VMEM((ROWS, COLS), BF16),
        pltpu.VMEM((COLS, COLS), F32),
        pltpu.VMEM((COLS, COLS), F32),
        pltpu.VMEM((2, 2, 2, 2, HALF, COLS), BF16),
        pltpu.VMEM((16, 2, 2, HALF, 128), BF16),
        pltpu.VMEM((2, 3, 2, COLS, COLS), BF16),
        pltpu.VMEM((2, 3, 64, COLS), BF16),
        pltpu.VMEM((2, 3, 64, COLS), BF16),
        pltpu.VMEM((2, 3, 64, COLS), F32),
        pltpu.VMEM((2, 3, 64, COLS), BF16),
        dma((10,)),
        *[dma((3,))] * 2,
        *[dma((2,))] * 2,
        *[dma((3, 4))] * 2,
        *[dma((7,))] * 2,
        *[dma((7,))] * 2,
        *[dma((3, 8))] * 2,
        *[dma((3,))] * 2,
        *[dma((2,))] * 2,
        *[dma((1,))] * 2,
        *[dma((2, 3))] * 2,
        *[dma((2, 4, 2, CHUNKS))] * 8,
    ]
    iso_rows, env_rows = pl.pallas_call(
        kernel,
        out_shape=(
            jax.ShapeDtypeStruct((2, 16, COLS), BF16),
            jax.ShapeDtypeStruct((2, 3, 64, COLS), BF16),
        ),
        in_specs=[anywhere] * 5,
        out_specs=(anywhere, anywhere),
        scratch_shapes=scratch,
        compiler_params=pltpu.CompilerParams(
            collective_id=0, has_side_effects=True, vmem_limit_bytes=60 * 2**20
        ),
        cost_estimate=pl.CostEstimate(flops=8 * 10**9, bytes_accessed=8 * 2**20, transcendentals=0),
        name="dmrg_window",
    )(shift_map.T, live_rows, wave_in, left_env, right_env.swapaxes(2, 3))
    return iso_rows, env_rows.swapaxes(2, 3)


def solution(mesh):
    split = Mesh(mesh.devices.reshape(NY, NX, NZ, 2), ("sector", *TERM))
    return jax.shard_map(
        body,
        mesh=split,
        in_specs=(
            P("sector", None, None),
            P("sector", TERM, None, None),
            P("sector", TERM, None, None),
            P(),
            P(),
        ),
        out_specs=(P("sector", TERM, None), P("sector", TERM, None, None)),
        check_vma=False,
    )
```
